32 devices in a mesh: head: 4 (over y, x), dp: 8 (over z, core).
Axes of the slice: x: 2, y: 2, z: 4, core: 2. Of those that a mesh axis runs over, the one named last changes fastest.
Arguments:
- block_in: bfloat16 [8, 2, 1024, 768], P('dp', None, 'head'), may hold values from -6 to 6
- ln_gains: float32 [2, 768], replicated, may hold values from 0.25 to 1.75
- ln_biases: float32 [2, 768], replicated, may hold values from -1.75 to 1.75
- w_qkv: bfloat16 [3, 768, 768], P(None, None, 'head'), may hold values from -0.21875 to 0.21875
- feat_maps: bfloat16 [2, 12, 64, 64], P(None, 'head'), may hold values from -1.5 to 1.5
- w_out: bfloat16 [768, 768], P('head'), may hold values from -0.875 to 0.875
- w_up: bfloat16 [768, 3072], P(None, 'head'), may hold values from -0.21875 to 0.21875
- w_down: bfloat16 [3072, 768], P('head'), may hold values from -0.109375 to 0.109375
- seq_lengths: int32 [8, 2, 2], P('dp'), may hold values from 0 to 1024, as said below
- out_cotangent: bfloat16 [8, 2, 1024, 768], P('dp', None, 'head'), may hold values from -6 to 6
Outputs:
- block_out: bfloat16 [8, 2, 1024, 768], P('dp', None, 'head')
- grad_in: float32 [8, 2, 1024, 768], P('dp', None, 'head')
- grad_ln_gains: float32 [2, 768], replicated
- grad_ln_biases: float32 [2, 768], replicated
- grad_w_qkv: float32 [3, 768, 768], P(None, None, 'head')
- grad_feat_maps: float32 [2, 12, 64, 64], P(None, 'head')
- grad_w_out: float32 [768, 768], P('head')
- grad_w_up: float32 [768, 3072], P(None, 'head')
- grad_w_down: float32 [3072, 768], P('head')
The draws below stay inside these ranges and needn't reach their ends.
Inputs may be any that keep to these rules, and one draw needn't show every extreme that they name: `seq_lengths`: entry [g, m] is either (1024, 0): one sequence, or (512, 512): two sequences; every group has micro-batches of both kinds.
All inputs are finite; a program needn't handle non-finite values.
Results may differ from the reference program's by a relative error of at most 0.018.
Values may be sent and summed in bfloat16 or wider, within the bound.
No kernel may reach another device: no remote copies, remote signals or barrier semaphores. Data moves between devices by JAX's collectives and lax.ppermute only.
A program may use at most 192 MiB of HBM per device.

```python
import jax
import jax.numpy as jnp
from jax import lax

D = 768
HEADS = 12
HD = 64
FF = 3072
MROWS = 1024
BLOCK = 256
MICRO = 2
GROUPS = 8


def draw_seq_lengths(key, part):
    key_flags, key_first, key_second = jax.random.split(jax.random.fold_in(key, 7), 3)
    flags = jax.random.randint(key_flags, (GROUPS, MICRO), 0, 2)
    first_long = jax.random.randint(key_first, (GROUPS, 1), 0, MICRO)
    second_pair = (first_long + 1 + jax.random.randint(key_second, (GROUPS, 1), 0, MICRO - 1)) % MICRO
    positions = jnp.arange(MICRO)[None, :]
    flags = jnp.where(positions == first_long, 0, jnp.where(positions == second_pair, 1, flags))
    half_rows = MROWS // 2
    leading = jnp.where(flags == 1, half_rows, MROWS)
    trailing = jnp.where(flags == 1, half_rows, 0)
    return jnp.stack([leading, trailing], axis=-1).astype(jnp.int32)


def block_scale(key, extent, pieces, smallest, largest):
    loudness, own = 1.0, jax.random.fold_in(key, 6)
    for axis_at, parts in pieces:
        heights = jnp.exp(jax.random.uniform(jax.random.fold_in(own, axis_at), (parts,), jnp.float32, smallest / len(pieces), largest / len(pieces)))
        loudness = loudness * jnp.repeat(heights, extent[axis_at] // parts).reshape([-1 if axis == axis_at else 1 for axis in range(len(extent))])
    return loudness


def normal_values(key, extent, deviation, bound, shards=(), kind=jnp.bfloat16):
    array = deviation * jax.random.normal(key, extent, jnp.float32)
    if shards:
        array = array * block_scale(key, extent, shards, -0.22, 0.18)
    return jnp.clip(array, -bound, bound).astype(kind)


def setup_inputs(seed: int = 0) -> dict:
    splits = jax.random.split(jax.random.key(seed), 11)
    return {
        "block_in": normal_values(splits[0], (GROUPS, MICRO, MROWS, D), 1.0, 6.0, ((0, 8), (2, 4))),
        "ln_gains": jnp.clip(1.0 + 0.15 * jax.random.normal(splits[1], (2, D), jnp.float32), 0.25, 1.75),
        "ln_biases": normal_values(splits[2], (2, D), 0.3, 1.75, (), jnp.float32),
        "w_qkv": normal_values(splits[3], (3, D, D), D ** -0.5, 0.21875, ((2, 4),)),
        "feat_maps": normal_values(splits[4], (2, HEADS, HD, HD), (HD // 4) ** -0.5, 1.5, ((1, 4),)),
        "w_out": normal_values(splits[5], (D, D), (D // 16) ** -0.5, 0.875, ((0, 4),)),
        "w_up": normal_values(splits[6], (D, FF), D ** -0.5, 0.21875, ((1, 4),)),
        "w_down": normal_values(splits[7], (FF, D), FF ** -0.5, 0.109375, ((0, 4),)),
        "seq_lengths": draw_seq_lengths(jax.random.fold_in(splits[10], 71), 0),
        "out_cotangent": normal_values(splits[9], (GROUPS, MICRO, MROWS, D), 1.0, 6.0, ((0, 8), (2, 4))),
    }


HIGHEST = lax.Precision.HIGHEST

@jax.custom_vjp
def low(v):
    return lax.optimization_barrier(v.astype(jnp.bfloat16)).astype(jnp.float32)

@jax.custom_vjp
def low_back(v):
    return v

def low_keep(v):
    return (low(v), None)

def low_pass(kept, grad):
    return (grad,)

def back_keep(v):
    return (v, None)

def back_low(kept, grad):
    return (low(grad),)
low.defvjp(low_keep, low_pass)
low_back.defvjp(back_keep, back_low)

def layer_norm(values, gain, bias):
    center = lax.optimization_barrier(jnp.mean(values, axis=-1, keepdims=True))
    shifted = values - center
    spread = lax.optimization_barrier(jnp.mean(shifted * shifted, axis=-1, keepdims=True))
    return shifted * lax.rsqrt(spread + 1e-05) * gain + bias

def features(values, feat_map):
    logits = low_back(jnp.einsum('hrd,hde->hre', values, feat_map, precision=HIGHEST))
    return jax.nn.softmax(jnp.concatenate([logits, -logits], axis=-1), axis=-1)

def to_blocks(values, block_count):
    head_count, row_total, feat_width = values.shape
    return values.reshape(head_count, block_count, row_total // block_count, feat_width).transpose(1, 0, 2, 3)

def from_blocks(values):
    block_count, head_count, block_rows, feat_width = values.shape
    return values.transpose(1, 0, 2, 3).reshape(head_count, block_count * block_rows, feat_width)

def lower_mask(block_rows):
    return (jnp.arange(block_rows)[:, None] >= jnp.arange(block_rows)[None, :]).astype(jnp.float32)

def block_step(carried, inputs):
    kv_state, key_sum = carried
    query_block, key_block, value_block, keep_flag = inputs
    kv_state = kv_state * keep_flag
    key_sum = key_sum * keep_flag
    causal = lower_mask(query_block.shape[1])
    scores = jnp.einsum('hqf,hkf->hqk', query_block, key_block, precision=HIGHEST) * causal
    prob_low = low(low_back(scores))
    numerator = low_back(jnp.einsum('hqk,hkd->hqd', prob_low, value_block, precision=HIGHEST) + jnp.einsum('hqf,hfd->hqd', query_block, kv_state, precision=HIGHEST))
    denominator = lax.optimization_barrier(jnp.sum(prob_low, axis=-1)) + jnp.einsum('hqf,hf->hq', query_block, key_sum, precision=HIGHEST)
    result = numerator / denominator[..., None]
    new_state = kv_state + jnp.einsum('hkf,hkd->hfd', key_block, value_block, precision=HIGHEST)
    new_sum = key_sum + lax.optimization_barrier(jnp.sum(key_block, axis=1))
    return ((new_state, new_sum), result)

def block_forward(rows_in, seq_lens, ln_gains, ln_biases, w_qkv, feat_maps, w_out, w_up, w_down):
    row_total = rows_in.shape[0]
    normed1 = low(layer_norm(rows_in, ln_gains[0], ln_biases[0]))
    projected = low(low_back(jnp.einsum('rd,cde->cre', normed1, w_qkv, precision=HIGHEST)))
    heads_split = projected.reshape(3, row_total, HEADS, HD).transpose(0, 2, 1, 3)
    phi_q = low(features(heads_split[0], feat_maps[0]))
    phi_k = low(features(heads_split[1], feat_maps[1]))
    block_count = row_total // BLOCK
    starts = jnp.arange(block_count, dtype=jnp.int32) * BLOCK
    resets = (starts == 0) | (seq_lens[1] > 0) & (starts == seq_lens[0])
    keep_flags = 1.0 - resets.astype(jnp.float32)
    initial = (jnp.zeros((HEADS, 2 * HD, HD), jnp.float32), jnp.zeros((HEADS, 2 * HD), jnp.float32))
    blocked = (to_blocks(phi_q, block_count), to_blocks(phi_k, block_count), to_blocks(heads_split[2], block_count), keep_flags)
    _, results = lax.scan(jax.checkpoint(block_step), initial, blocked)
    mixed = low(from_blocks(results).transpose(1, 0, 2).reshape(row_total, HEADS * HD))
    attn_out = low_back(jnp.dot(mixed, w_out, precision=HIGHEST))
    residual = rows_in + attn_out
    normed2 = low(layer_norm(residual, ln_gains[1], ln_biases[1]))
    up_proj = low_back(jnp.dot(normed2, w_up, precision=HIGHEST))
    hidden = low(jax.nn.gelu(up_proj, approximate=True))
    mlp_out = low_back(jnp.dot(hidden, w_down, precision=HIGHEST))
    return residual + mlp_out

def reference(block_in, ln_gains, ln_biases, w_qkv, feat_maps, w_out, w_up, w_down, seq_lengths, out_cotangent):
    params = (ln_gains.astype(jnp.float32), ln_biases.astype(jnp.float32), w_qkv.astype(jnp.float32), feat_maps.astype(jnp.float32), w_out.astype(jnp.float32), w_up.astype(jnp.float32), w_down.astype(jnp.float32))
    full_shape = block_in.shape
    flat_count = full_shape[0] * full_shape[1]
    flat_in = block_in.reshape(flat_count, MROWS, D).astype(jnp.float32)
    flat_lens = seq_lengths.reshape(flat_count, 2)
    flat_grad = out_cotangent.reshape(flat_count, MROWS, D).astype(jnp.float32)

    def advance(totals, inputs):
        rows_in, seq_lens, grad_rows = inputs

        def forward(values, *weights):
            return block_forward(values, seq_lens, *weights)
        result, pullback = jax.vjp(forward, rows_in, *params)
        gradients = pullback(grad_rows)
        totals = jax.tree.map(jnp.add, totals, tuple(gradients[1:]))
        return (totals, (result.astype(jnp.bfloat16), gradients[0]))
    initial = jax.tree.map(jnp.zeros_like, params)
    totals, (outputs, input_grads) = lax.scan(advance, initial, (flat_in, flat_lens, flat_grad))
    return (outputs.reshape(full_shape), input_grads.reshape(full_shape), totals[0], totals[1], totals[2], totals[3], totals[4], totals[5], totals[6])
```

```python
from functools import partial

import jax
import jax.numpy as jnp
from jax import lax
from jax.experimental import pallas as pl
from jax.experimental.pallas import tpu as pltpu
from jax.sharding import PartitionSpec as P

BF = jnp.bfloat16
F32 = jnp.float32
AXES = ("head", "dp")
SLOTS = 4
LANES = 128
EPS = 1e-05
SIGMA = (0, 2, 1, 3)

NN = (((1,), (0,)), ((), ()))
NT = (((1,), (1,)), ((), ()))
TN = (((0,), (0,)), ((), ()))


def mm(a, b, dims=NN):
    return lax.dot_general(a, b, dims, preferred_element_type=F32)


def lane_low(shape):
    return lax.broadcasted_iota(jnp.int32, shape, 1) < 64


def norm_parts(v):
    center = jnp.mean(v, axis=-1, keepdims=True)
    shifted = v - center
    spread = jnp.mean(shifted * shifted, axis=-1, keepdims=True)
    inverse = lax.rsqrt(spread + EPS)
    return shifted * inverse, inverse


def norm_back(a, n, inverse, gain):
    e = a * gain
    m1 = jnp.mean(e, axis=-1, keepdims=True)
    m2 = jnp.mean(e * n, axis=-1, keepdims=True)
    return inverse * (e - m1 - n * m2)


def full(shape):
    return pl.BlockSpec(shape, lambda i: (0,) * len(shape))


def part(shape, *at):
    return pl.BlockSpec(shape, lambda i: at)


SMEM = pl.BlockSpec(memory_space=pltpu.SMEM)


def call(body, in_specs, outs, out_specs=None, scratch=(), flops=0, nbytes=0, alias=None):
    return pl.pallas_call(
        body,
        grid=(1,),
        in_specs=in_specs,
        out_specs=out_specs or [full(o[0]) for o in outs],
        out_shape=[jax.ShapeDtypeStruct(*o) for o in outs],
        scratch_shapes=list(scratch),
        input_output_aliases=alias or {},
        compiler_params=pltpu.CompilerParams(vmem_limit_bytes=56 * 1024 * 1024),
        cost_estimate=pl.CostEstimate(flops=flops, bytes_accessed=nbytes, transcendentals=0),
    )


def norm_kernel(x_ref, gain_ref, bias_ref, out_ref):
    n, _ = norm_parts(x_ref[...].astype(F32))
    out_ref[...] = (n * gain_ref[0:1, :] + bias_ref[0:1, :]).astype(BF)


def unpack_feat(block):
    return jnp.concatenate([block[:, i * LANES : (i + 1) * LANES] for i in range(6)], axis=0)


def head_map(feat, h):
    a = feat[h * 64 : (h + 1) * 64, :].astype(F32)
    low = lane_low(a.shape)
    turned = pltpu.roll(a, 64, 1)
    top = jnp.where(low, a, -turned)
    bottom = jnp.where(low, turned, -a)
    zero = jnp.zeros_like(a)
    return jnp.concatenate(
        [jnp.concatenate([top, zero], axis=1), jnp.concatenate([zero, bottom], axis=1)], axis=0
    ).astype(BF)


def softmax_rows(z):
    e = jnp.exp(z - jnp.max(z, axis=-1, keepdims=True))
    return e * (1.0 / jnp.sum(e, axis=-1, keepdims=True))


def causal(rows):
    return lax.broadcasted_iota(jnp.int32, (rows, rows), 0) >= lax.broadcasted_iota(
        jnp.int32, (rows, rows), 1
    )


def with_ones(v):
    return jnp.concatenate([v, jnp.ones_like(v)], axis=1)


def first_kernel(rows, micro, heads, meta, n1, wo, wt, fo, qkv, phq, phk, acc, st, wbuf):
    half = wo.shape[0]
    c = meta[0]
    wbuf[pl.ds(pl.multiple_of(c * half, 32), half), :] = wo[...]
    wbuf[pl.ds(pl.multiple_of((1 - c) * half, 32), half), :] = wt[...]
    qkv[...] = mm(n1[...], wbuf[...], NT).astype(BF)
    feat = unpack_feat(fo[...])
    mask = causal(rows)
    for h in range(heads):
        fmap = head_map(feat, h)
        hl = slice(h * LANES, (h + 1) * LANES)
        for m in range(micro):
            rs = slice(m * rows, (m + 1) * rows)
            z = mm(qkv[rs, hl], fmap)
            pq = softmax_rows(z[:, :LANES]).astype(BF)
            pk = softmax_rows(z[:, LANES:]).astype(BF)
            phq[rs, hl] = pq
            phk[rs, hl] = pk
            v0 = heads * LANES + h * 64
            v1 = with_ones(qkv[rs, v0 : v0 + 64])
            prob = jnp.where(mask, mm(pq, pk, NT), 0.0).astype(BF)
            acc[rs, hl] = mm(prob, v1)
            lt = mm(v1, pk, TN)
            put_state(st, m, h, heads, lt)


def put_state(st, m, h, heads, lt):
    st[m, h * 64 : (h + 1) * 64, :] = lt[:64].astype(BF)
    base = heads * 64
    row = lax.broadcasted_iota(jnp.int32, (16, LANES), 0)
    mine = jnp.where(row == h, lt[64:80], 0.0)
    if h == 0:
        st[m, base : base + 16, :] = mine.astype(BF)
    else:
        st[m, base : base + 16, :] = (st[m, base : base + 16, :].astype(F32) + mine).astype(BF)


def take_state(s, h, heads):
    row = s[heads * 64 + h : heads * 64 + h + 1, :]
    return jnp.concatenate(
        [s[h * 64 : (h + 1) * 64, :], jnp.broadcast_to(row, (64, LANES))], axis=0
    ).astype(BF)


def joined(meta, k, m, r1, r2, r3):
    keep = (1 - meta[4 + m]).astype(F32)
    a = r1[k ^ meta[2], m].astype(F32)
    b = r2[k ^ meta[3], m].astype(F32) + r3[k ^ 3, m].astype(F32)
    return a + keep * b


def mix_kernel(rows, micro, heads, meta, x, gain, bias, r1, r2, r3, *refs):
    accs, phqs, wos, wts = refs[0:4], refs[4:8], refs[8:12], refs[12:16]
    mixed, iden, ust, resid, n2, wbuf = refs[16:]
    gather_out(meta, wos, wts, wbuf)
    low = lane_low((rows, LANES))
    for m in range(micro):
        rs = slice(m * rows, (m + 1) * rows)
        for k in range(SLOTS):
            s = joined(meta, k, m, r1, r2, r3)
            ust[k, m] = s.astype(BF)
            for h in range(heads):
                i = k * heads + h
                hl = slice(h * LANES, (h + 1) * LANES)
                a = accs[k][rs, hl] + mm(phqs[k][rs, hl], take_state(s, h, heads), NT)
                turned = pltpu.roll(a, 64, 1)
                if i % 2 == 0:
                    inv0 = 1.0 / turned
                    mix0 = a * inv0
                else:
                    inv1 = 1.0 / a
                    mix1 = turned * inv1
                    cl = slice((i // 2) * LANES, (i // 2 + 1) * LANES)
                    mixed[rs, cl] = jnp.where(low, mix0, mix1).astype(BF)
                    iden[rs, cl] = jnp.where(low, inv0, inv1)
    res = x[...].astype(F32) + mm(mixed[...], wbuf[...])
    resid[...] = res
    n, _ = norm_parts(res)
    n2[...] = (n * gain[1:2, :] + bias[1:2, :]).astype(BF)


def gather_out(meta, wos, wts, wbuf):
    half = wos[0].shape[0]
    c = meta[0]
    for k in range(SLOTS):
        base = k * 2 * half
        wbuf[pl.ds(pl.multiple_of(base + c * half, 32), half), :] = wos[k][...]
        wbuf[pl.ds(pl.multiple_of(base + (1 - c) * half, 32), half), :] = wts[k][...]


def gelu_parts(u):
    a = 0.7978845608028654
    u2 = u * u
    t = jnp.tanh(a * u * (1.0 + 0.044715 * u2))
    half = 0.5 * (1.0 + t)
    return u * half, half + 0.5 * u * (1.0 - t * t) * a * (1.0 + 3 * 0.044715 * u2)


def mlp_kernel(tile, first, n2, g, wo, wt, *refs):
    if first:
        keep, send, mo, dn, wu, wd = refs
    else:
        mo_in, dn_in, keep, send, mo, dn, wu, wd = refs
    half = wo.shape[0] // 2
    wu[:half, :] = wo[:half, :]
    wu[half:, :] = wt[:half, :]
    wd[:half, :] = wo[half:, :]
    wd[half:, :] = wt[half:, :]
    for t in range(2 * half // tile):
        rs = slice(t * tile, (t + 1) * tile)
        up = mm(n2[...], wu[rs, :], NT)
        hid, slope = gelu_parts(up)
        hid = hid.astype(BF)
        dup = (mm(g[...], wd[rs, :], NT) * slope).astype(BF)
        a = mm(hid, wd[rs, :])
        b = mm(dup, wu[rs, :])
        if t:
            mo[...] += a
            dn[...] += b
        elif first:
            mo[...] = a
            dn[...] = b
        else:
            mo[...] = mo_in[...] + a
            dn[...] = dn_in[...] + b
        gu = mm(dup, n2[...], TN).astype(BF)
        gd = mm(hid, g[...], TN).astype(BF)
        lo, hi = t * tile, (t + 1) * tile
        if lo < half:
            e = min(hi, half)
            keep[lo:e, :] = gu[: e - lo]
            keep[half + lo : half + e, :] = gd[: e - lo]
        if hi > half:
            s = max(lo, half)
            send[s - half : hi - half, :] = gu[s - lo :]
            send[s : hi, :] = gd[s - lo :]


def turn_kernel(rows, micro, heads, meta, resid, mo, dn, g, gain, mixed, iden, *refs):
    phqs, wos, wts = refs[0:4], refs[4:8], refs[8:12]
    out, dres, dnx, gwo, hst, dln, wbuf, dmix = refs[12:]
    gather_out(meta, wos, wts, wbuf)
    out[...] = (resid[...] + mo[...]).astype(BF)
    n, inverse = norm_parts(resid[...])
    a = dn[...]
    dr = g[...].astype(F32) + norm_back(a, n, inverse, gain[1:2, :])
    dres[...] = dr
    dln[0:1, :] = jnp.sum(a * n, axis=0, keepdims=True)
    dln[1:2, :] = jnp.sum(a, axis=0, keepdims=True)
    dat = dr.astype(BF)
    gwo[...] = mm(mixed[...], dat, TN).astype(BF)
    dmix[...] = mm(dat, wbuf[...], NT)
    low = lane_low((rows, LANES))
    for m in range(micro):
        rs = slice(m * rows, (m + 1) * rows)
        for j in range(SLOTS * heads // 2):
            cl = slice(j * LANES, (j + 1) * LANES)
            d, iv = dmix[rs, cl], iden[rs, cl]
            t = d * mixed[rs, cl].astype(F32)
            even = jnp.sum(jnp.where(low, t, 0.0), axis=-1, keepdims=True)
            odd = jnp.sum(jnp.where(low, 0.0, t), axis=-1, keepdims=True)
            dn_ = d * iv
            x0 = jnp.where(low, dn_, even * (-1.0 / 64) * pltpu.roll(iv, 64, 1)).astype(BF)
            x1 = jnp.where(low, pltpu.roll(dn_, 64, 1), odd * (-1.0 / 64) * iv).astype(BF)
            for i, xv in ((2 * j, x0), (2 * j + 1, x1)):
                k, h = divmod(i, heads)
                hl = slice(h * LANES, (h + 1) * LANES)
                dnx[rs, i * LANES : (i + 1) * LANES] = xv
                put_state(hst.at[k], m, h, heads, mm(xv, phqs[k][rs, hl], TN))


def last_kernel(rows, micro, heads, first, k, meta, qkv, phq, phk, dnx, ust, h1, h2, h3, wo, wt, fo, n1, gwo, *refs):
    if first:
        keep, send, dn1, wbuf, dproj, ww, gw = refs
    else:
        dn1_in, keep, send, dn1, wbuf, dproj, ww, gw = refs
    half = wo.shape[0]
    c = meta[0]
    wbuf[pl.ds(pl.multiple_of(c * half, 32), half), :] = wo[...]
    wbuf[pl.ds(pl.multiple_of((1 - c) * half, 32), half), :] = wt[...]
    feat = unpack_feat(fo[...])
    mask = causal(rows)
    feat_grads = []
    vbase = heads * LANES
    for h in range(heads):
        fmap = head_map(feat, h)
        hl = slice(h * LANES, (h + 1) * LANES)
        for m in range(micro):
            rs = slice(m * rows, (m + 1) * rows)
            pq, pk, dx = phq[rs, hl], phk[rs, hl], dnx[rs, hl]
            v1 = with_ones(qkv[rs, vbase + h * 64 : vbase + h * 64 + 64])
            prob = jnp.where(mask, mm(pq, pk, NT), 0.0).astype(BF)
            ds = jnp.where(mask, mm(dx, v1, NT), 0.0).astype(BF)
            ux = take_state(ust[0, m], h, heads)
            hx = take_state(joined(meta, k, m, h1, h2, h3), h, heads)
            dpq = mm(ds, pk) + mm(dx, ux)
            dpk = mm(ds, pq, TN) + mm(v1, hx)
            dv = mm(prob, dx, TN) + mm(pk, hx, NT)
            pqf, pkf = pq.astype(F32), pk.astype(F32)
            wq = pqf * (dpq - jnp.sum(pqf * dpq, axis=-1, keepdims=True))
            wk = pkf * (dpk - jnp.sum(pkf * dpk, axis=-1, keepdims=True))
            wqk = jnp.concatenate([wq, wk], axis=1).astype(BF)
            ww[rs, :] = wqk
            dproj[rs, hl] = mm(wqk, fmap, NT).astype(BF)
            dproj[rs, vbase + h * 64 : vbase + h * 64 + 64] = dv[:, :64].astype(BF)
        g = mm(qkv[:, hl], ww[...], TN)
        top, bottom = g[:64], g[64:]
        gq = top[:, :LANES] - pltpu.roll(top[:, :LANES], 64, 1)
        gk = bottom[:, LANES:] - pltpu.roll(bottom[:, LANES:], 64, 1)
        feat_grads.append(jnp.where(lane_low(gq.shape), gq, -gk))
    if first:
        dn1[...] = mm(dproj[...], wbuf[...])
    else:
        dn1[...] = dn1_in[...] + mm(dproj[...], wbuf[...])
    gw[...] = mm(dproj[...], n1[...], TN).astype(BF)
    keep[0:half, :] = gw[pl.ds(pl.multiple_of(c * half, 32), half), :]
    send[0:half, :] = gw[pl.ds(pl.multiple_of((1 - c) * half, 32), half), :]
    oh = gwo.shape[0] // 2
    keep[half : half + oh, :] = gwo[pl.ds(pl.multiple_of(c * oh, 32), oh), :]
    send[half : half + oh, :] = gwo[pl.ds(pl.multiple_of((1 - c) * oh, 32), oh), :]
    fg = jnp.concatenate(feat_grads, axis=0)
    fg = jnp.concatenate([fg[i * 32 : (i + 1) * 32] for i in range(6)], axis=1)
    top, bottom = fg[:16], fg[16:]
    is0 = c == 0
    keep[half + oh :, :] = jnp.where(is0, top, bottom).astype(BF)
    send[half + oh :, :] = jnp.where(is0, bottom, top).astype(BF)


def end_kernel(x, dn1, dres, gain, gin, dln):
    n, inverse = norm_parts(x[...].astype(F32))
    a = dn1[...]
    gin[...] = dres[...] + norm_back(a, n, inverse, gain[0:1, :])
    dln[0:1, :] = jnp.sum(a * n, axis=0, keepdims=True)
    dln[1:2, :] = jnp.sum(a, axis=0, keepdims=True)


def links(heads_axis, dp):
    def table(fn):
        return [(r * dp + d, q[0] * dp + q[1]) for r in range(heads_axis) for d in range(dp) for q in [fn(r, d)] if q]

    one = table(lambda r, d: (r ^ (1 + d % 2), d))
    two = table(lambda r, d: (r ^ (2 - d % 2), d))
    head = {b: table(lambda r, d: (r ^ b, d)) for b in (1, 2)}
    later = {b: table(lambda r, d: (r ^ b, d) if r < r ^ b else None) for b in (1, 2, 3)}
    early = {b: table(lambda r, d: (r ^ b, d) if r > r ^ b else None) for b in (1, 2, 3)}
    bits = {}
    b = 1
    while b < dp:
        bits[b] = table(lambda r, d: (r, d ^ b))
        b *= 2
    return one, two, head, later, early, bits


def move(v, table):
    return lax.ppermute(v, AXES, table)


def all_sum(total, zbit, bits):
    rows = total.shape[0] // 2
    mine = lax.dynamic_slice_in_dim(total, zbit * rows, rows, 0)
    other = lax.dynamic_slice_in_dim(total, (1 - zbit) * rows, rows, 0)
    a = mine + move(other, bits[2])
    for b in sorted(bits):
        if b > 2:
            a = a + move(a, bits[b])
    return a, move(a, bits[2])


def in_order(first, a, b):
    return jnp.where(first == 0, jnp.concatenate([a, b]), jnp.concatenate([b, a]))


def local(heads_axis, dp, block_in, ln_gains, ln_biases, w_qkv, feat_maps, w_out, w_up, w_down, seq_lengths, out_cotangent):
    one, two, head, later, early, bits = links(heads_axis, dp)
    micro, rows, width = block_in.shape[1:]
    tokens = micro * rows
    heads = feat_maps.shape[1]
    ff = w_up.shape[1]
    hidden = heads * 64
    rank, dpi = lax.axis_index("head"), lax.axis_index("dp")
    core, zbit = dpi % 2, (dpi // 2) % 2
    splits = (seq_lengths[0, :, 1] > 0).astype(jnp.int32)
    meta = jnp.concatenate(
        [jnp.stack([core, rank, 1 + core, 2 - core]).astype(jnp.int32), splits]
    )

    x = block_in.reshape(tokens, width)
    g = out_cotangent.reshape(tokens, width)

    wt = jnp.swapaxes(w_qkv, 1, 2)
    qk = wt[:2].reshape(2, heads, 64, width).swapaxes(0, 1).reshape(2 * hidden, width)
    wqkv = jnp.concatenate([qk, wt[2]])
    feats = feat_maps.transpose(1, 2, 0, 3).reshape(6, 32, LANES).transpose(1, 0, 2).reshape(32, width)
    qrows, orows = 3 * hidden // 2, hidden // 2
    pair = jnp.concatenate(
        [wqkv.reshape(2, qrows, width), w_out.reshape(2, orows, width), jnp.stack([feats, feats])], axis=1
    )
    arows = pair.shape[1]
    a_own = [lax.dynamic_index_in_dim(pair, core, 0, False)]
    a_oth = [lax.dynamic_index_in_dim(pair, 1 - core, 0, False)]
    a_own += [move(a_own[0], one), move(a_own[0], two)]
    a_own += [move(a_own[1], two)]
    a_oth += [move(a_own[SIGMA[k]], bits[1]) for k in (1, 2, 3)]

    pair = jnp.concatenate([w_up.T.reshape(2, ff // 2, width), w_down.reshape(2, ff // 2, width)], axis=1)
    b_own = [lax.dynamic_index_in_dim(pair, core, 0, False)]
    b_oth = [lax.dynamic_index_in_dim(pair, 1 - core, 0, False)]
    b_own += [move(b_own[0], one), move(b_own[0], two)]
    b_own += [move(b_own[1], two)]
    b_oth += [move(b_own[SIGMA[k]], bits[1]) for k in (1, 2, 3)]

    tw = (tokens, width)
    ln_spec = full(ln_gains.shape)
    n1 = call(norm_kernel, [full(tw), ln_spec, ln_spec], [(tw, BF)])(x, ln_gains, ln_biases)[0]

    wl = heads * LANES
    srows = hidden + 16
    st_shape = (micro, srows, LANES)
    st_all = (SLOTS,) + st_shape
    qspec, ospec = part((qrows, width), 0, 0), part((orows, width), qrows // orows, 0)
    fspec = part((32, width), (qrows + orows) // 32, 0)
    qw = 3 * hidden
    slots = []
    for k in range(SLOTS):
        slots.append(
            call(
                partial(first_kernel, rows, micro, heads),
                [SMEM, full(tw), qspec, qspec, fspec],
                [((tokens, qw), BF), ((tokens, wl), BF), ((tokens, wl), BF), ((tokens, wl), F32), (st_shape, BF)],
                scratch=[pltpu.VMEM((2 * qrows, width), BF)],
                flops=5 * 10**9,
                nbytes=5 * 10**6,
            )(meta, n1, a_own[k], a_oth[k], a_own[k])
        )
    qkvs, phqs, phks, accs, sts = zip(*slots)
    states = jnp.stack(sts)
    recv = [move(states, later[b]) for b in (1, 2, 3)]
    mixed, iden, ust, resid, n2 = call(
        partial(mix_kernel, rows, micro, heads),
        [SMEM, full(tw), ln_spec, ln_spec] + [full(st_all)] * 3 + [full((tokens, wl))] * 8 + [ospec] * 8,
        [(tw, BF), (tw, F32), (st_all, BF), (tw, F32), (tw, BF)],
        scratch=[pltpu.VMEM((SLOTS * hidden, width), BF)],
        flops=5 * 10**9,
        nbytes=15 * 10**6,
    )(meta, x, ln_gains, ln_biases, *recv, *accs, *phqs, *a_own, *a_oth)

    keeps, sends = [None] * SLOTS, [None] * SLOTS
    sums = ()
    for k in (0, 1, 3, 2):
        keeps[k], sends[k], *sums = call(
            partial(mlp_kernel, 256, not sums),
            [full(tw), full(tw), full((ff, width)), full((ff, width))] + [full(tw)] * len(sums),
            [((ff, width), BF), ((ff, width), BF), (tw, F32), (tw, F32)],
            scratch=[pltpu.VMEM((ff, width), BF)] * 2,
            flops=6 * 2 * tokens * width * ff,
            nbytes=12 * 10**6,
        )(n2, g, b_own[k], b_oth[k], *sums)
    mo, dn = sums
    mlp_half = reduce_plane(keeps, sends, one, two, bits)
    mlp_sum = all_sum(mlp_half, zbit, bits)

    out, dres, dnx, gwo, hst, dln2 = call(
        partial(turn_kernel, rows, micro, heads),
        [SMEM, full(tw), full(tw), full(tw), full(tw), ln_spec, full(tw), full(tw)]
        + [full((tokens, wl))] * 4
        + [ospec] * 8,
        [(tw, BF), (tw, F32), ((tokens, SLOTS * wl), BF), ((SLOTS * hidden, width), BF), (st_all, BF), ((2, width), F32)],
        scratch=[pltpu.VMEM((SLOTS * hidden, width), BF), pltpu.VMEM(tw, F32)],
        flops=5 * 10**9,
        nbytes=15 * 10**6,
    )(meta, resid, mo, dn, g, ln_gains, mixed, iden, *phqs, *a_own, *a_oth)
    hrecv = [move(hst, early[b]) for b in (1, 2, 3)]

    grows = qrows + orows + 16
    keeps, sends = [None] * SLOTS, [None] * SLOTS
    dn1 = ()
    for k in (1, 3, 2, 0):
        keeps[k], sends[k], *dn1 = call(
            partial(last_kernel, rows, micro, heads, not dn1, k),
            [
                SMEM,
                full((tokens, qw)),
                full((tokens, wl)),
                full((tokens, wl)),
                part((tokens, wl), 0, k),
                part((1,) + st_shape, k, 0, 0, 0),
            ]
            + [full(st_all)] * 3
            + [qspec, qspec, fspec, full(tw), part((hidden, width), k, 0)]
            + [full(tw)] * len(dn1),
            [((grows, width), BF), ((grows, width), BF), (tw, F32)],
            scratch=[
                pltpu.VMEM((2 * qrows, width), BF),
                pltpu.VMEM((tokens, qw), BF),
                pltpu.VMEM((tokens, 2 * LANES), BF),
                pltpu.VMEM((2 * qrows, width), BF),
            ],
            flops=8 * 10**9,
            nbytes=12 * 10**6,
        )(meta, qkvs[k], phqs[k], phks[k], dnx, ust, *hrecv, a_own[k], a_oth[k], a_own[k], n1, gwo, *dn1)
    attn_half = reduce_plane(keeps, sends, one, two, bits)
    attn_sum = all_sum(attn_half, zbit, bits)

    gin, dln1 = call(
        end_kernel,
        [full(tw), full(tw), full(tw), ln_spec],
        [(tw, F32), ((2, width), F32)],
    )(x, dn1[0], dres, ln_gains)
    lns = jnp.concatenate([dln1, dln2])
    for b in (1, 2):
        lns = lns + move(lns, head[b])
    for b in sorted(bits):
        lns = lns + move(lns, bits[b])

    def whole(pair):
        mine = in_order(zbit, *pair)
        other = move(mine, bits[1])
        return mine, other

    mine, other = whole(mlp_sum)
    fh = ff // 2
    gup = in_order(core, mine[:fh], other[:fh]).astype(F32).T
    gdown = in_order(core, mine[fh:], other[fh:]).astype(F32)
    mine, other = whole(attn_sum)
    gq = in_order(core, mine[:qrows], other[:qrows]).astype(F32)
    gqk = gq[: 2 * hidden].reshape(heads, 2, 64, width).swapaxes(0, 1).reshape(2, hidden, width)
    gqkv = jnp.concatenate([gqk, gq[None, 2 * hidden :]]).swapaxes(1, 2)
    gout = in_order(core, mine[qrows : qrows + orows], other[qrows : qrows + orows]).astype(F32)
    gf = in_order(core, mine[qrows + orows :], other[qrows + orows :]).astype(F32)
    gf = gf.reshape(32, 6, LANES).transpose(1, 0, 2).reshape(heads, 64, 2, 64).transpose(2, 0, 1, 3)
    shape = (1, micro, rows, width)
    return (
        out.reshape(shape),
        gin.reshape(shape),
        jnp.stack([lns[0], lns[2]]),
        jnp.stack([lns[1], lns[3]]),
        gqkv,
        gf,
        gout,
        gup,
        gdown,
    )


def reduce_plane(keeps, sends, one, two, bits):
    s = [keeps[k] + move(sends[SIGMA[k]], bits[1]) for k in range(SLOTS)]
    s0 = s[0] + move(s[1], one)
    s2 = s[2] + move(s[3], one)
    return s0 + move(s2, two)


def solution(mesh):
    return jax.shard_map(
        partial(local, mesh.shape["head"], mesh.shape["dp"]),
        mesh=mesh,
        in_specs=(
            P("dp", None, "head", None),
            P(),
            P(),
            P(None, None, "head"),
            P(None, "head", None, None),
            P("head", None),
            P(None, "head"),
            P("head", None),
            P("dp", None, None),
            P("dp", None, "head", None),
        ),
        out_specs=(
            P("dp", None, "head", None),
            P("dp", None, "head", None),
            P(),
            P(),
            P(None, None, "head"),
            P(None, "head", None, None),
            P("head", None),
            P(None, "head"),
            P("head", None),
        ),
        check_vma=False,
    )
```

```python
from functools import partial

import jax
import jax.numpy as jnp
from jax import lax
from jax.experimental import pallas as pl
from jax.experimental.pallas import tpu as pltpu
from jax.sharding import PartitionSpec as P

BF = jnp.bfloat16
F32 = jnp.float32
AXES = ("head", "dp")
SLOTS = 4
LANES = 128
EPS = 1e-05
SIGMA = (0, 2, 1, 3)

NN = (((1,), (0,)), ((), ()))
NT = (((1,), (1,)), ((), ()))
TN = (((0,), (0,)), ((), ()))


def mm(a, b, dims=NN):
    return lax.dot_general(a, b, dims, preferred_element_type=F32)


def lane_low(shape):
    return lax.broadcasted_iota(jnp.int32, shape, 1) < 64


def norm_parts(v):
    center = jnp.mean(v, axis=-1, keepdims=True)
    shifted = v - center
    spread = jnp.mean(shifted * shifted, axis=-1, keepdims=True)
    inverse = lax.rsqrt(spread + EPS)
    return shifted * inverse, inverse


def norm_back(a, n, inverse, gain):
    e = a * gain
    m1 = jnp.mean(e, axis=-1, keepdims=True)
    m2 = jnp.mean(e * n, axis=-1, keepdims=True)
    return inverse * (e - m1 - n * m2)


VMEM = pl.BlockSpec(memory_space=pltpu.VMEM)
SMEM = pl.BlockSpec(memory_space=pltpu.SMEM)
ANY = pl.BlockSpec(memory_space=pl.ANY)


SCALE = 100


class Order:
    def __init__(self):
        self.last = None

    def __call__(self, body, args, outs, scratch=(), after=(), alias=None, limit=24, meta=True, us=1.0):
        deps = list(after) + ([] if self.last is None else [self.last])
        n, nd = len(args), len(deps)

        def run(*refs):
            body(*refs[:n], *refs[n + nd :])

        res = pl.pallas_call(
            run,
            in_specs=([SMEM] if meta else []) + [VMEM] * (n - meta) + [ANY] * nd,
            out_specs=[VMEM] * len(outs),
            out_shape=[jax.ShapeDtypeStruct(*o) for o in outs],
            scratch_shapes=list(scratch),
            input_output_aliases=alias or {},
            compiler_params=pltpu.CompilerParams(vmem_limit_bytes=limit * 1024 * 1024),
            name=getattr(body, "func", body).__name__,
            cost_estimate=pl.CostEstimate(
                flops=int(16 * 1.15e9), bytes_accessed=1000, transcendentals=0
            ),
        )(*args, *deps)
        self.last = res[0]
        return res

    def add(self, *terms):
        return self(add_kernel, list(terms), [(terms[0].shape, terms[0].dtype)], meta=False)[0]

    def gate(self, *arrays):
        n = len(arrays)
        res = self(gate_kernel, list(arrays), [(a.shape, a.dtype) for a in arrays], meta=False)
        return res if n > 1 else res[0]

    def pause(self):
        (out,) = self(pause_kernel, [], [((8, LANES), F32)], meta=False)
        return out


def gate_kernel(*refs):
    n = len(refs) // 2
    for a, out in zip(refs[:n], refs[n:]):
        out[...] = a[...]


def pause_kernel(out):
    out[...] = jnp.zeros_like(out)


def add_kernel(*refs):
    *terms, out = refs
    total = terms[0][...].astype(F32)
    for t in terms[1:]:
        total = total + t[...].astype(F32)
    out[...] = total.astype(out.dtype)


def pack_kernel(heads, wqkv, wout, feats, out):
    hidden = heads * 64
    for h in range(heads):
        for c in range(2):
            at = h * LANES + c * 64
            out[at : at + 64, :] = wqkv[c, h * 64 : (h + 1) * 64, :]
    out[2 * hidden : 3 * hidden, :] = wqkv[2]
    out[3 * hidden : 4 * hidden, :] = wout[...]
    both = [jnp.concatenate([feats[0, h], feats[1, h]], axis=1) for h in range(heads)]
    both = jnp.concatenate(both, axis=0)
    out[4 * hidden :, :] = jnp.concatenate([both[i * 32 : (i + 1) * 32] for i in range(6)], axis=1)


def turn_over_kernel(a, *outs):
    for i, out in enumerate(outs):
        n = out.shape[0]
        out[...] = a[:, i * n : (i + 1) * n].T


def copy_kernel(a, *outs):
    at = 0
    for out in outs:
        out[...] = a[at : at + out.shape[0], :]
        at += out.shape[0]


def pick_half_kernel(meta, a, out):
    half = out.shape[0]
    out[...] = a[pl.ds(pl.multiple_of(meta[0] * half, 16), half), :]


def pick_kernel(meta, *refs):
    n = len(refs) // 3
    for i in range(n):
        refs[2 * n + i][...] = jnp.where(meta[0] == 0, refs[2 * i][...], refs[2 * i + 1][...])


def unpack_feat(block):
    return jnp.concatenate([block[:, i * LANES : (i + 1) * LANES] for i in range(6)], axis=0)


def head_map(feat, h):
    a = feat[h * 64 : (h + 1) * 64, :].astype(F32)
    low = lane_low(a.shape)
    turned = pltpu.roll(a, 64, 1)
    top = jnp.where(low, a, -turned)
    bottom = jnp.where(low, turned, -a)
    zero = jnp.zeros_like(a)
    return jnp.concatenate(
        [jnp.concatenate([top, zero], axis=1), jnp.concatenate([zero, bottom], axis=1)], axis=0
    ).astype(BF)


def softmax_rows(z):
    e = jnp.exp(z - jnp.max(z, axis=-1, keepdims=True))
    return e * (1.0 / jnp.sum(e, axis=-1, keepdims=True))


def causal(rows):
    return lax.broadcasted_iota(jnp.int32, (rows, rows), 0) >= lax.broadcasted_iota(
        jnp.int32, (rows, rows), 1
    )


def with_ones(v):
    return jnp.concatenate([v, jnp.ones_like(v)], axis=1)


def joined_halves(c, own, other, out):
    half = own.shape[0]
    out[pl.ds(pl.multiple_of(c * half, 16), half), :] = own[...]
    out[pl.ds(pl.multiple_of((1 - c) * half, 16), half), :] = other[...]


def first_kernel(k, rows, micro, heads, meta, *refs):
    if k == 0:
        x, gain, bias, w, n1, qkv, phq, phk, acc, st = refs
        n, _ = norm_parts(x[...].astype(F32))
        n1[...] = (n * gain[0:1, :] + bias[0:1, :]).astype(BF)
    elif k < 3:
        n1, w, _, qkv, phq, phk, acc, st = refs
    else:
        n1, own, other, _, w, qkv, phq, phk, acc, st = refs
        joined_halves(meta[0], own, other, w)
    st = st.at[k]
    hidden = heads * 64
    qkv[...] = mm(n1[...], w[: 3 * hidden, :], NT).astype(BF)
    feat = unpack_feat(w[4 * hidden :, :])
    mask = causal(rows)
    for h in range(heads):
        fmap = head_map(feat, h)
        hl = slice(h * LANES, (h + 1) * LANES)
        for m in range(micro):
            rs = slice(m * rows, (m + 1) * rows)
            z = mm(qkv[rs, hl], fmap)
            pq = softmax_rows(z[:, :LANES]).astype(BF)
            pk = softmax_rows(z[:, LANES:]).astype(BF)
            phq[rs, hl] = pq
            phk[rs, hl] = pk
            v0 = heads * LANES + h * 64
            v1 = with_ones(qkv[rs, v0 : v0 + 64])
            prob = jnp.where(mask, mm(pq, pk, NT), 0.0).astype(BF)
            acc[rs, hl] = mm(prob, v1)
            put_state(st, m, h, heads, mm(v1, pk, TN))


def put_state(st, m, h, heads, lt):
    st[m, h * 64 : (h + 1) * 64, :] = lt[:64].astype(BF)
    base = heads * 64
    row = lax.broadcasted_iota(jnp.int32, (16, LANES), 0)
    mine = jnp.where(row == h, lt[64:80], 0.0)
    if h == 0:
        st[m, base : base + 16, :] = mine.astype(BF)
    else:
        st[m, base : base + 16, :] = (st[m, base : base + 16, :].astype(F32) + mine).astype(BF)


def take_state(s, h, heads):
    row = s[heads * 64 + h : heads * 64 + h + 1, :]
    return jnp.concatenate(
        [s[h * 64 : (h + 1) * 64, :], jnp.broadcast_to(row, (64, LANES))], axis=0
    ).astype(BF)


def relay_kernel(at, micro, meta, own, got, out):
    for m in range(micro):
        f = [meta[at + 4 * m + i].astype(F32) for i in range(2)]
        for k in range(SLOTS):
            out[k, m] = (f[0] * own[k, m].astype(F32) + f[1] * got[k ^ 1, m].astype(F32)).astype(BF)


def joined(at, meta, k, m, r1, r2):
    f = [meta[at + 4 * m + i].astype(F32) for i in (2, 3)]
    return f[0] * r1[k ^ 1, m].astype(F32) + f[1] * r2[k ^ 2, m].astype(F32)


def mix_kernel(rows, micro, heads, at, meta, x, gain, bias, r1, r2, *refs):
    accs, phqs, ws = refs[0:4], refs[4:8], refs[8:12]
    mixed, iden, ust, resid, n2 = refs[12:]
    hidden = heads * 64
    low = lane_low((rows, LANES))
    for m in range(micro):
        rs = slice(m * rows, (m + 1) * rows)
        for k in range(SLOTS):
            s = joined(at, meta, k, m, r1, r2)
            ust[k, m] = s.astype(BF)
            for h in range(heads):
                i = k * heads + h
                hl = slice(h * LANES, (h + 1) * LANES)
                a = accs[k][rs, hl] + mm(phqs[k][rs, hl], take_state(s, h, heads), NT)
                turned = pltpu.roll(a, 64, 1)
                if i % 2 == 0:
                    inv0 = 1.0 / turned
                    mix0 = a * inv0
                else:
                    inv1 = 1.0 / a
                    mix1 = turned * inv1
                    cl = slice((i // 2) * LANES, (i // 2 + 1) * LANES)
                    mixed[rs, cl] = jnp.where(low, mix0, mix1).astype(BF)
                    iden[rs, cl] = jnp.where(low, inv0, inv1)
    wo = jnp.concatenate([w[3 * hidden : 4 * hidden, :] for w in ws], axis=0)
    res = x[...].astype(F32) + mm(mixed[...], wo)
    resid[...] = res
    n, _ = norm_parts(res)
    n2[...] = (n * gain[1:2, :] + bias[1:2, :]).astype(BF)


def gelu_parts(u):
    a = 0.7978845608028654
    u2 = u * u
    t = jnp.tanh(a * u * (1.0 + 0.044715 * u2))
    half = 0.5 * (1.0 + t)
    return u * half, half + 0.5 * u * (1.0 - t * t) * a * (1.0 + 3 * 0.044715 * u2)


def mlp_kernel(k, first, meta, n2, g, u0, u1, d0, d1, *refs):
    if not first:
        mo_in, dn_in, *refs = refs
    keep, send, mo, dn = refs
    half = u0.shape[0]
    wu = jnp.concatenate([u0[...], u1[...]], axis=0)
    wd = jnp.concatenate([d0[...], d1[...]], axis=0)
    up = mm(n2[...], wu, NT)
    hid, slope = gelu_parts(up)
    hid = hid.astype(BF)
    dup = (mm(g[...], wd, NT) * slope).astype(BF)
    a = mm(hid, wd)
    b = mm(dup, wu)
    mo[...] = a if first else mo_in[...] + a
    dn[...] = b if first else dn_in[...] + b
    mine = (meta[0] == 0) if k < 3 else True
    for at, grad in ((0, mm(dup, n2[...], TN)), (half, mm(hid, g[...], TN))):
        grad = grad.astype(BF)
        top, bottom = grad[:half], grad[half:]
        keep[at : at + half, :] = top if k == 3 else jnp.where(mine, top, bottom)
        send[at : at + half, :] = bottom if k == 3 else jnp.where(mine, bottom, top)


def turn_kernel(rows, micro, heads, meta, resid, mo, dn, g, gain, mixed, iden, *refs):
    phqs, ws = refs[0:4], refs[4:8]
    out, dres, dnx, gwo, hst, dln, dmix = refs[8:]
    hidden = heads * 64
    out[...] = (resid[...] + mo[...]).astype(BF)
    n, inverse = norm_parts(resid[...])
    a = dn[...]
    dr = g[...].astype(F32) + norm_back(a, n, inverse, gain[1:2, :])
    dres[...] = dr
    dln[...] = jnp.zeros_like(dln)
    dln[0:1, :] = jnp.sum(a * n, axis=0, keepdims=True)
    dln[1:2, :] = jnp.sum(a, axis=0, keepdims=True)
    dat = dr.astype(BF)
    gwo[...] = mm(mixed[...], dat, TN).astype(BF)
    wo = jnp.concatenate([w[3 * hidden : 4 * hidden, :] for w in ws], axis=0)
    dmix[...] = mm(dat, wo, NT)
    low = lane_low((rows, LANES))
    for m in range(micro):
        rs = slice(m * rows, (m + 1) * rows)
        for j in range(SLOTS * heads // 2):
            cl = slice(j * LANES, (j + 1) * LANES)
            d, iv = dmix[rs, cl], iden[rs, cl]
            t = d * mixed[rs, cl].astype(F32)
            even = jnp.sum(jnp.where(low, t, 0.0), axis=-1, keepdims=True)
            odd = jnp.sum(jnp.where(low, 0.0, t), axis=-1, keepdims=True)
            dn_ = d * iv
            x0 = jnp.where(low, dn_, even * (-1.0 / 64) * pltpu.roll(iv, 64, 1)).astype(BF)
            x1 = jnp.where(low, pltpu.roll(dn_, 64, 1), odd * (-1.0 / 64) * iv).astype(BF)
            for i, xv in ((2 * j, x0), (2 * j + 1, x1)):
                k, h = divmod(i, heads)
                hl = slice(h * LANES, (h + 1) * LANES)
                dnx[rs, i * LANES : (i + 1) * LANES] = xv
                put_state(hst.at[k], m, h, heads, mm(xv, phqs[k][rs, hl], TN))


def back_kernel(k, rows, micro, heads, meta, qkv, phq, phk, dnx, ust, wq, dpk, dv):
    mask = causal(rows)
    vbase = heads * LANES
    for h in range(heads):
        hl = slice(h * LANES, (h + 1) * LANES)
        dl = slice((k * heads + h) * LANES, (k * heads + h + 1) * LANES)
        for m in range(micro):
            rs = slice(m * rows, (m + 1) * rows)
            pq, pk, dx = phq[rs, hl], phk[rs, hl], dnx[rs, dl]
            v1 = with_ones(qkv[rs, vbase + h * 64 : vbase + h * 64 + 64])
            prob = jnp.where(mask, mm(pq, pk, NT), 0.0).astype(BF)
            ds = jnp.where(mask, mm(dx, v1, NT), 0.0).astype(BF)
            dpq = mm(ds, pk) + mm(dx, take_state(ust[k, m], h, heads))
            pqf = pq.astype(F32)
            wq[rs, hl] = (pqf * (dpq - jnp.sum(pqf * dpq, axis=-1, keepdims=True))).astype(BF)
            dpk[rs, hl] = mm(ds, pq, TN)
            dv[rs, hl] = mm(prob, dx, TN)


def last_kernel(k, rows, micro, heads, at, first, final, meta, qkv, phk, wq, dpk, dv, h1, h2, w, n1, gwo, *refs):
    if not first:
        dn1_in, *refs = refs
    if final:
        x, dres, gain, dln2, *refs = refs
        keep, send, gin, dln, dproj, ww, gw, dn1 = refs
    else:
        keep, send, dn1, dproj, ww, gw = refs
    hidden = heads * 64
    c = meta[0]
    feat = unpack_feat(w[4 * hidden : 4 * hidden + 32, :])
    feat_grads = []
    vbase = heads * LANES
    sts = [joined(at, meta, k, m, h1, h2) for m in range(micro)]
    for h in range(heads):
        fmap = head_map(feat, h)
        hl = slice(h * LANES, (h + 1) * LANES)
        for m in range(micro):
            rs = slice(m * rows, (m + 1) * rows)
            pk = phk[rs, hl]
            v1 = with_ones(qkv[rs, vbase + h * 64 : vbase + h * 64 + 64])
            hx = take_state(sts[m], h, heads)
            dp = dpk[rs, hl] + mm(v1, hx)
            dval = dv[rs, hl] + mm(pk, hx, NT)
            pkf = pk.astype(F32)
            wk = (pkf * (dp - jnp.sum(pkf * dp, axis=-1, keepdims=True))).astype(BF)
            wqk = jnp.concatenate([wq[rs, hl], wk], axis=1)
            ww[rs, :] = wqk
            dproj[rs, hl] = mm(wqk, fmap, NT).astype(BF)
            dproj[rs, vbase + h * 64 : vbase + h * 64 + 64] = dval[:, :64].astype(BF)
        g = mm(qkv[:, hl], ww[...], TN)
        top, bottom = g[:64], g[64:]
        gq = top[:, :LANES] - pltpu.roll(top[:, :LANES], 64, 1)
        gk = bottom[:, LANES:] - pltpu.roll(bottom[:, LANES:], 64, 1)
        feat_grads.append(jnp.where(lane_low(gq.shape), gq, -gk))
    total = mm(dproj[...], w[: 3 * hidden, :])
    dn1[...] = total if first else dn1_in[...] + total
    gw[...] = mm(dproj[...], n1[...], TN).astype(BF)
    fg = jnp.concatenate(feat_grads, axis=0)
    fg = jnp.concatenate([fg[i * 32 : (i + 1) * 32] for i in range(6)], axis=1).astype(BF)
    qh, oh = 3 * hidden // 2, hidden // 2
    for out, at in ((keep, c), (send, 1 - c)):
        out[:qh, :] = gw[pl.ds(pl.multiple_of(at * qh, 16), qh), :]
        out[qh : qh + oh, :] = gwo[pl.ds(pl.multiple_of(k * hidden + at * oh, 16), oh), :]
        out[qh + oh : qh + oh + 16, :] = jnp.where(at == 0, fg[:16], fg[16:])
        out[qh + oh + 16 :, :] = jnp.zeros_like(fg[:16])
    if final:
        n, inverse = norm_parts(x[...].astype(F32))
        a = dn1[...]
        gin[...] = dres[...] + norm_back(a, n, inverse, gain[0:1, :])
        dln[8:, :] = dln2[...]
        dln[:8, :] = jnp.zeros_like(dln2)
        dln[0:1, :] = jnp.sum(a * n, axis=0, keepdims=True)
        dln[1:2, :] = jnp.sum(a, axis=0, keepdims=True)


def split_kernel(terms, parts, meta, *refs):
    if len(refs) > terms + 2 * parts:
        lns, *refs = refs
        *refs, buf = refs
        total = refs[0][...].astype(F32)
        for t in refs[1:terms]:
            total = total + t[...].astype(F32)
        buf[...] = total
        n = buf.shape[0]
        buf[n - 16 :, :] += lns[...]
        refs, terms = [buf, *refs[terms:]], 1
    arrays, outs = refs[:terms], refs[terms:]
    z = meta[1]
    n = outs[0].shape[0]
    for i, out in enumerate(outs):
        side = z if i < parts else 1 - z
        rs = pl.ds(pl.multiple_of(side * parts * n + (i % parts) * n, 16), n)
        total = arrays[0][rs, :].astype(F32)
        for t in arrays[1:]:
            total = total + t[rs, :].astype(F32)
        out[...] = total.astype(BF)


def finish_ff_kernel(parts, meta, *refs):
    *pieces, gup, gdown, buf = refs
    c, z = meta[0], meta[1]
    n = pieces[0].shape[0]
    half = parts * n
    i = 0
    for cc in (c, 1 - c):
        for zz in (z, 1 - z):
            for p in range(parts):
                at = zz * 2 * half + cc * half + p * n
                buf[pl.ds(pl.multiple_of(at, 16), n), :] = pieces[i][...]
                i += 1
    ff = gdown.shape[0]
    gup[...] = buf[:ff, :].astype(F32).T
    gdown[...] = buf[ff:, :].astype(F32)


def collect(meta, pieces, buf):
    c, z = meta[0], meta[1]
    quarter = pieces[0].shape[0]
    for piece, place in zip(pieces, (2 * c + z, 2 * c + 1 - z, 2 * (1 - c) + z, 2 * (1 - c) + 1 - z)):
        buf[pl.ds(pl.multiple_of(place * quarter, 16), quarter), :] = piece[...]


def finish_kernel(heads, meta, p0, p1, p2, p3, gqkv, gfeat, gout, gains, biases, buf):
    collect(meta, (p0, p1, p2, p3), buf)
    hidden = heads * 64
    half, qh, oh = buf.shape[0] // 2, 3 * hidden // 2, hidden // 2

    def rows(at, n, first, size):
        parts = []
        while n:
            c, inner = divmod(at, size)
            m = min(n, size - inner)
            parts.append(buf[c * half + first + inner : c * half + first + inner + m, :])
            at, n = at + m, n - m
        return jnp.concatenate(parts, axis=0) if len(parts) > 1 else parts[0]

    for h in range(heads):
        for c in range(2):
            gqkv[c, h * 64 : (h + 1) * 64, :] = rows(h * LANES + c * 64, 64, 0, qh).astype(F32)
    gqkv[2] = rows(2 * hidden, hidden, 0, qh).astype(F32)
    gout[...] = rows(0, hidden, qh, oh).astype(F32)
    feat = unpack_feat(rows(0, 32, qh + oh, 16)).astype(F32)
    for h in range(heads):
        gfeat[0, h] = feat[h * 64 : (h + 1) * 64, :64]
        gfeat[1, h] = feat[h * 64 : (h + 1) * 64, 64:]
    ln = buf[half - 16 : half, :].astype(F32) + buf[2 * half - 16 :, :].astype(F32)
    gains[0:1, :] = ln[0:1]
    gains[1:2, :] = ln[8:9]
    biases[0:1, :] = ln[1:2]
    biases[1:2, :] = ln[9:10]


def links(heads_axis, dp):
    def table(fn):
        return [(r * dp + d, q[0] * dp + q[1]) for r in range(heads_axis) for d in range(dp) for q in [fn(r, d)] if q]

    one = table(lambda r, d: (r ^ (1 + d % 2), d))
    two = table(lambda r, d: (r ^ (2 - d % 2), d))
    head = {b: table(lambda r, d: (r ^ b, d)) for b in (1, 2)}
    bits = {}
    b = 1
    while b < dp:
        bits[b] = table(lambda r, d: (r, d ^ b))
        b *= 2
    return one, two, head, bits


def move(v, table, name="move"):
    with jax.named_scope(name):
        return lax.ppermute(v, AXES, table)


def factors(r, core, keep):
    high, odd = r // 2, r % 2
    first = [jnp.ones_like(r), jnp.ones_like(r), odd, high * keep]
    second = [1 - high * odd, keep * high, keep * high, jnp.minimum(r, 1)]
    return [jnp.where(core == 0, a, b) for a, b in zip(first, second)]


def local(heads_axis, dp, block_in, ln_gains, ln_biases, w_qkv, feat_maps, w_out, w_up, w_down, seq_lengths, out_cotangent):
    one, two, head, bits = links(heads_axis, dp)
    micro, rows, width = block_in.shape[1:]
    tokens = micro * rows
    heads = feat_maps.shape[1]
    ff = w_up.shape[1]
    hidden = heads * 64
    rank, dpi = lax.axis_index("head"), lax.axis_index("dp")
    core, zbit = dpi % 2, (dpi // 2) % 2
    keeps = [1 - (seq_lengths[0, m, 1] > 0).astype(jnp.int32) for m in range(micro)]
    scalars = [core, zbit]
    for r in (rank, 3 - rank):
        for m in range(micro):
            scalars += factors(r, core, keeps[m])
    meta = jnp.stack([jnp.asarray(v, jnp.int32) for v in scalars])
    fwd, bwd = 2, 2 + 4 * micro

    x = block_in.reshape(tokens, width)
    g = out_cotangent.reshape(tokens, width)
    tw = (tokens, width)

    arows, half = 4 * hidden + 32, ff // 2
    call = Order()
    swap = lambda v, name="swap": move(v, bits[1], name)
    piece = ((half, width), BF)

    (a0,) = call(partial(pack_kernel, heads), [jnp.swapaxes(w_qkv, 1, 2), w_out, feat_maps], [((arows, width), BF)], meta=False)
    a1 = move(a0, one, "a1")
    u0, u1 = call(turn_over_kernel, [w_up], [piece] * 2, meta=False)
    bu0 = move(u0, one, "bu0")

    wl, qw = heads * LANES, 3 * hidden
    st_all = (SLOTS, micro, hidden + 16, LANES)
    first_outs = [((tokens, qw), BF), ((tokens, wl), BF), ((tokens, wl), BF), ((tokens, wl), F32), (st_all, BF)]
    first = lambda k: partial(first_kernel, k, rows, micro, heads)
    slots = []

    def attend(k, w):
        slots.append(call(first(k), [meta, n1, w, slots[-1][4]], first_outs, alias={3: 4}))

    n1, *slot = call(first(0), [meta, x, ln_gains, ln_biases, a0], [(tw, BF)] + first_outs)
    slots.append(slot)
    a1 = call.gate(a1)
    a2 = swap(a1, "a2")
    (asl,) = call(pick_half_kernel, [meta, a1], [((arows // 2, width), BF)])
    ahalf = move(asl, two, "ahalf")
    u1 = call.gate(u1)
    bu1 = move(u1, one, "bu1")
    d0, d1 = call(copy_kernel, [w_down], [piece] * 2, meta=False)
    attend(1, a1)
    a2, bu0, d0 = call.gate(a2, bu0, d0)
    b2u0 = swap(bu0, "b2u0")
    bd0 = move(d0, one, "bd0")
    attend(2, a2)
    ahalf, b2u0 = call.gate(ahalf, b2u0)
    aother = swap(ahalf, "aother")
    call.pause()
    a3, *slot = call(
        first(3), [meta, n1, ahalf, aother, slots[-1][4]], [((arows, width), BF)] + first_outs, alias={4: 5}
    )
    slots.append(slot)
    ws = [a0, a1, a2, a3]
    qkvs, phqs, phks, accs, sts = zip(*slots)

    r1 = move(sts[-1], one, "r1")
    bu1 = call.gate(bu1)
    b2u1 = swap(bu1, "b2u1")
    (du,) = call(pick_kernel, [meta, bu0, bu1], [piece])
    (on,) = call(partial(relay_kernel, fwd, micro), [meta, sts[-1], r1], [(st_all, BF)])
    r2 = move(on, two, "r2")
    bd0, b2u1 = call.gate(bd0, b2u1)
    b2d0 = swap(bd0, "b2d0")
    call.pause()
    r2, d1 = call.gate(r2, d1)
    bd1 = move(d1, one, "bd1")
    b2d0 = call.gate(b2d0)
    mixed, iden, ust, resid, n2 = call(
        partial(mix_kernel, rows, micro, heads, fwd),
        [meta, x, ln_gains, ln_biases, r1, r2, *accs, *phqs, *ws],
        [(tw, BF), (tw, F32), (st_all, BF), (tw, F32), (tw, BF)],
    )

    keeps, sends = [None] * SLOTS, [None] * SLOTS
    sums = []

    def mlp(k, *w):
        keeps[k], sends[k], *sums[:] = call(
            partial(mlp_kernel, k, not sums),
            [meta, n2, g, *w, *sums],
            [((ff, width), BF), ((ff, width), BF), (tw, F32), (tw, F32)],
            alias={7: 2, 8: 3} if sums else None,
        )
        return swap(sends[k], "got%d" % k)

    got0 = mlp(0, u0, u1, d0, d1)
    bd1, du = call.gate(bd1, du)
    b2d1 = swap(bd1, "b2d1")
    du = move(du, two, "du")
    (dd,) = call(pick_kernel, [meta, bd0, bd1], [piece])
    dd = move(dd, two, "dd")
    s0 = call.add(keeps[0], got0)
    got1 = mlp(1, bu0, bu1, bd0, bd1)
    got2 = mlp(2, b2u0, b2u1, b2d0, b2d1)
    s2 = call.add(keeps[2], got1)
    s1 = call.add(keeps[1], got2)
    one1 = move(s1, one, "one1")
    du, dd = call.gate(du, dd)
    du2, dd2 = swap(du, "du2"), swap(dd, "dd2")
    call.pause()
    got3 = mlp(3, du, du2, dd, dd2)
    mo, dn = sums

    out, dres, dnx, gwo, hst, dln2 = call(
        partial(turn_kernel, rows, micro, heads),
        [meta, resid, mo, dn, g, ln_gains, mixed, iden, *phqs, *ws],
        [(tw, BF), (tw, F32), ((tokens, SLOTS * wl), BF), ((SLOTS * hidden, width), BF), (st_all, BF), ((8, width), F32)],
        scratch=[pltpu.VMEM(tw, F32)],
    )
    h1 = move(hst, one, "h1")
    one1 = call.gate(one1)
    s3 = call.add(keeps[3], got3)
    one3 = move(s3, one, "one3")
    backs = []
    for k in range(SLOTS):
        if k == 3:
            (on,) = call(partial(relay_kernel, bwd, micro), [meta, hst, h1], [(st_all, BF)])
            h2 = move(on, two, "h2")
        backs.append(
            call(
                partial(back_kernel, k, rows, micro, heads),
                [meta, qkvs[k], phqs[k], phks[k], dnx, ust],
                [((tokens, wl), BF), ((tokens, wl), F32), ((tokens, wl), F32)],
            )
        )

    grows = arows + 32
    akeeps, asends = [None] * SLOTS, [None] * SLOTS
    dn1 = []

    def last(k):
        final = k == 0
        args = [meta, qkvs[k], phks[k], *backs[k], h1, h2, ws[k], n1, gwo, *dn1]
        outs = [((grows // 2, width), BF)] * 2
        scratch = [pltpu.VMEM((tokens, qw), BF), pltpu.VMEM((tokens, 2 * LANES), BF), pltpu.VMEM((qw, width), BF)]
        akeeps[k], asends[k], *dn1[:] = call(
            partial(last_kernel, k, rows, micro, heads, bwd, not dn1, final),
            args + ([x, dres, ln_gains, dln2] if final else []),
            outs + ([(tw, F32), ((16, width), F32)] if final else [(tw, F32)]),
            scratch=scratch + ([pltpu.VMEM(tw, F32)] if final else []),
            alias={11: 2} if dn1 and not final else None,
        )
        return swap(asends[k], "agot%d" % k)

    h2 = call.gate(h2)
    s2 = call.add(s2, one3)
    two2 = move(s2, two, "two2")
    agot3 = last(3)
    agot1 = last(1)
    t3 = call.add(akeeps[3], agot3)
    aone3 = move(t3, one, "aone3")
    agot2 = last(2)
    t2 = call.add(akeeps[2], agot1)
    agot0 = last(0)
    gin, lns = dn1
    ln1 = move(lns, head[1], "ln1")
    t1 = call.add(akeeps[1], agot2)
    aone1 = move(t1, one, "aone1")
    t2 = call.add(t2, aone3)
    atwo2 = move(t2, two, "atwo2")
    t0 = call.add(akeeps[0], agot0)

    def split(terms, parts, name, extra=()):
        n, w = terms[0].shape
        shapes = [((n // 2 // parts, w), BF)] * (2 * parts)
        scratch = [pltpu.VMEM((n, w), F32)] if extra else []
        res = call(partial(split_kernel, len(terms), parts), [meta, *extra, *terms], shapes, scratch=scratch)
        return [(res[i], move(res[parts + i], bits[2], name)) for i in range(parts)]

    def over(pieces, b, name):
        return [(p, move(p, bits[b], name)) for p in pieces]

    zs = [b for b in sorted(bits) if b > 2]
    ffs = split([s0, one1, two2], 2, "zf")
    lns = call.add(lns, ln1)
    ln2 = move(lns, head[2], "ln2")
    lead = zs[0] if zs else None
    if zs:
        ffs[0] = over([call.add(*ffs[0])], lead, "yf")[0]
    lns = call.add(lns, ln2)
    ats = split([t0, aone1, atwo2], 1, "za", [lns])
    if zs:
        ffs[1] = over([call.add(*ffs[1])], lead, "yf")[0]
        ats[0] = over([call.add(*ats[0])], lead, "ya")[0]
    for b in zs[1:]:
        for i in range(2):
            ffs[i] = over([call.add(*ffs[i])], b, "yf")[0]
        ats[0] = over([call.add(*ats[0])], b, "ya")[0]
    mine, theirs, fms, fts = [None] * 2, [None] * 2, [None] * 2, [None] * 2
    for i in range(2):
        mine[i] = call.add(*ffs[i])
        theirs[i] = move(mine[i], bits[2], "xf")
        fms[i] = swap(mine[i], "fm%d" % i)
    theirs[0] = call.gate(theirs[0])
    fts[0] = swap(theirs[0], "ft0")
    amine = call.add(*ats[0])
    atheirs = move(amine, bits[2], "xa")
    am = swap(amine, "am")
    theirs[1] = call.gate(theirs[1])
    fts[1] = swap(theirs[1], "ft1")
    call.pause()
    gup, gdown = call(
        partial(finish_ff_kernel, 2),
        [meta, *mine, *theirs, *fms, *fts],
        [((width, ff), F32), ((ff, width), F32)],
        scratch=[pltpu.VMEM((2 * ff, width), BF)],
    )
    atheirs = call.gate(atheirs)
    at = swap(atheirs, "at")
    call.pause()
    gqkv, gfeat, gout, gains, biases = call(
        partial(finish_kernel, heads),
        [meta, amine, atheirs, am, at],
        [((3, hidden, width), F32), (feat_maps.shape, F32), (w_out.shape, F32), (ln_gains.shape, F32), (ln_biases.shape, F32)],
        scratch=[pltpu.VMEM((grows, width), BF)],
    )
    gqkv = jnp.swapaxes(gqkv, 1, 2)
    shape = (1, micro, rows, width)
    return (out.reshape(shape), gin.reshape(shape), gains, biases, gqkv, gfeat, gout, gup, gdown)


def solution(mesh):
    return jax.shard_map(
        partial(local, mesh.shape["head"], mesh.shape["dp"]),
        mesh=mesh,
        in_specs=(
            P("dp", None, "head", None),
            P(),
            P(),
            P(None, None, "head"),
            P(None, "head", None, None),
            P("head", None),
            P(None, "head"),
            P("head", None),
            P("dp", None, None),
            P("dp", None, "head", None),
        ),
        out_specs=(
            P("dp", None, "head", None),
            P("dp", None, "head", None),
            P(),
            P(),
            P(None, None, "head"),
            P(None, "head", None, None),
            P("head", None),
            P(None, "head"),
            P("head", None),
        ),
        check_vma=False,
    )
```

```python
from functools import partial

import jax
import jax.numpy as jnp
from jax import lax
from jax.experimental import pallas as pl
from jax.experimental.pallas import tpu as pltpu
from jax.sharding import PartitionSpec as P

BF = jnp.bfloat16
F32 = jnp.float32
AXES = ("head", "dp")
SLOTS = 4
LANES = 128
EPS = 1e-05
SIGMA = (0, 2, 1, 3)

NN = (((1,), (0,)), ((), ()))
NT = (((1,), (1,)), ((), ()))
TN = (((0,), (0,)), ((), ()))


def mm(a, b, dims=NN):
    return lax.dot_general(a, b, dims, preferred_element_type=F32)


def lane_low(shape):
    return lax.broadcasted_iota(jnp.int32, shape, 1) < 64


def norm_parts(v):
    center = jnp.mean(v, axis=-1, keepdims=True)
    shifted = v - center
    spread = jnp.mean(shifted * shifted, axis=-1, keepdims=True)
    inverse = lax.rsqrt(spread + EPS)
    return shifted * inverse, inverse


def norm_back(a, n, inverse, gain):
    e = a * gain
    m1 = jnp.mean(e, axis=-1, keepdims=True)
    m2 = jnp.mean(e * n, axis=-1, keepdims=True)
    return inverse * (e - m1 - n * m2)


VMEM = pl.BlockSpec(memory_space=pltpu.VMEM)
SMEM = pl.BlockSpec(memory_space=pltpu.SMEM)
ANY = pl.BlockSpec(memory_space=pl.ANY)


SCALE = 100


class Order:
    def __init__(self):
        self.last = None

    def __call__(self, body, args, outs, scratch=(), after=(), alias=None, limit=8, meta=True, us=1.0):
        deps = list(after) + ([] if self.last is None else [self.last])
        n, nd = len(args), len(deps)

        def run(*refs):
            body(*refs[:n], *refs[n + nd :])

        res = pl.pallas_call(
            run,
            in_specs=([SMEM] if meta else []) + [VMEM] * (n - meta) + [ANY] * nd,
            out_specs=[VMEM] * len(outs),
            out_shape=[jax.ShapeDtypeStruct(*o) for o in outs],
            scratch_shapes=list(scratch),
            input_output_aliases=alias or {},
            compiler_params=pltpu.CompilerParams(vmem_limit_bytes=limit * 1024 * 1024),
            name=getattr(body, "func", body).__name__,
            cost_estimate=pl.CostEstimate(
                flops=int(16 * 1.15e9), bytes_accessed=1000, transcendentals=0
            ),
        )(*args, *deps)
        self.last = res[0]
        return res

    def add(self, *terms):
        return self(add_kernel, list(terms), [(terms[0].shape, terms[0].dtype)], meta=False)[0]

    def gate(self, *arrays):
        n = len(arrays)
        res = self(gate_kernel, list(arrays), [(a.shape, a.dtype) for a in arrays], meta=False)
        return res if n > 1 else res[0]

    def pause(self):
        (out,) = self(pause_kernel, [], [((8, LANES), F32)], meta=False)
        return out


def gate_kernel(*refs):
    n = len(refs) // 2
    for a, out in zip(refs[:n], refs[n:]):
        out[...] = a[...]


def add_norms_kernel(lns, more, *refs):
    add_kernel(*refs)
    out = refs[-1]
    rows = out.shape[0] - lns.shape[0]
    out[rows:, :] = (lns[...] + more[...]).astype(BF)


def pause_kernel(out):
    out[...] = jnp.zeros_like(out)


def add_kernel(*refs):
    *terms, out = refs
    total = terms[0][...].astype(F32)
    for t in terms[1:]:
        total = total + t[...].astype(F32)
    out[...] = total.astype(out.dtype)


def pack_kernel(heads, wqkv, wout, feats, out):
    hidden = heads * 64
    for h in range(heads):
        for c in range(2):
            at = h * LANES + c * 64
            out[at : at + 64, :] = wqkv[c, h * 64 : (h + 1) * 64, :]
    out[2 * hidden : 3 * hidden, :] = wqkv[2]
    out[3 * hidden : 4 * hidden, :] = wout[...]
    both = [jnp.concatenate([feats[0, h], feats[1, h]], axis=1) for h in range(heads)]
    both = jnp.concatenate(both, axis=0)
    out[4 * hidden :, :] = jnp.concatenate([both[i * 32 : (i + 1) * 32] for i in range(6)], axis=1)


def turn_over_kernel(a, *outs):
    for i, out in enumerate(outs):
        n = out.shape[0]
        out[...] = a[:, i * n : (i + 1) * n].T


def copy_kernel(a, *outs):
    at = 0
    for out in outs:
        out[...] = a[at : at + out.shape[0], :]
        at += out.shape[0]


def pick_half_kernel(meta, a, out):
    half = out.shape[0]
    out[...] = a[pl.ds(pl.multiple_of(meta[0] * half, 16), half), :]


def pick_kernel(meta, *refs):
    n = len(refs) // 3
    for i in range(n):
        refs[2 * n + i][...] = jnp.where(meta[0] == 0, refs[2 * i][...], refs[2 * i + 1][...])


def unpack_feat(block):
    return jnp.concatenate([block[:, i * LANES : (i + 1) * LANES] for i in range(6)], axis=0)


def head_map(feat, h):
    a = feat[h * 64 : (h + 1) * 64, :].astype(F32)
    low = lane_low(a.shape)
    turned = pltpu.roll(a, 64, 1)
    top = jnp.where(low, a, -turned)
    bottom = jnp.where(low, turned, -a)
    zero = jnp.zeros_like(a)
    return jnp.concatenate(
        [jnp.concatenate([top, zero], axis=1), jnp.concatenate([zero, bottom], axis=1)], axis=0
    ).astype(BF)


def softmax_rows(z):
    e = jnp.exp(z - jnp.max(z, axis=-1, keepdims=True))
    return e * (1.0 / jnp.sum(e, axis=-1, keepdims=True))


def causal(rows):
    return lax.broadcasted_iota(jnp.int32, (rows, rows), 0) >= lax.broadcasted_iota(
        jnp.int32, (rows, rows), 1
    )


def with_ones(v):
    return jnp.concatenate([v, jnp.ones_like(v)], axis=1)


def joined_halves(c, own, other, out):
    half = own.shape[0]
    out[pl.ds(pl.multiple_of(c * half, 16), half), :] = own[...]
    out[pl.ds(pl.multiple_of((1 - c) * half, 16), half), :] = other[...]


def first_kernel(k, rows, micro, heads, meta, *refs):
    if k == 0:
        x, gain, bias, w, n1, qkv, phq, phk, acc, st = refs
        n, _ = norm_parts(x[...].astype(F32))
        n1[...] = (n * gain[0:1, :] + bias[0:1, :]).astype(BF)
    elif k < 3:
        n1, w, _, qkv, phq, phk, acc, st = refs
    else:
        n1, own, other, _, w, qkv, phq, phk, acc, st = refs
        joined_halves(meta[0], own, other, w)
    st = st.at[k]
    hidden = heads * 64
    qkv[...] = mm(n1[...], w[: 3 * hidden, :], NT).astype(BF)
    feat = unpack_feat(w[4 * hidden :, :])
    mask = causal(rows)
    for h in range(heads):
        fmap = head_map(feat, h)
        hl = slice(h * LANES, (h + 1) * LANES)
        for m in range(micro):
            rs = slice(m * rows, (m + 1) * rows)
            z = mm(qkv[rs, hl], fmap)
            pq = softmax_rows(z[:, :LANES]).astype(BF)
            pk = softmax_rows(z[:, LANES:]).astype(BF)
            phq[rs, hl] = pq
            phk[rs, hl] = pk
            v0 = heads * LANES + h * 64
            v1 = with_ones(qkv[rs, v0 : v0 + 64])
            prob = jnp.where(mask, mm(pq, pk, NT), 0.0).astype(BF)
            acc[rs, hl] = mm(prob, v1)
            put_state(st, m, h, heads, mm(v1, pk, TN))


def put_state(st, m, h, heads, lt):
    st[m, h * 64 : (h + 1) * 64, :] = lt[:64].astype(BF)
    base = heads * 64
    row = lax.broadcasted_iota(jnp.int32, (16, LANES), 0)
    mine = jnp.where(row == h, lt[64:80], 0.0)
    if h == 0:
        st[m, base : base + 16, :] = mine.astype(BF)
    else:
        st[m, base : base + 16, :] = (st[m, base : base + 16, :].astype(F32) + mine).astype(BF)


def take_state(s, h, heads):
    row = s[heads * 64 + h : heads * 64 + h + 1, :]
    return jnp.concatenate(
        [s[h * 64 : (h + 1) * 64, :], jnp.broadcast_to(row, (64, LANES))], axis=0
    ).astype(BF)


def relay_kernel(at, micro, meta, own, got, out):
    for m in range(micro):
        f = [meta[at + 4 * m + i].astype(F32) for i in range(2)]
        for k in range(SLOTS):
            out[k, m] = (f[0] * own[k, m].astype(F32) + f[1] * got[k ^ 1, m].astype(F32)).astype(BF)


def joined(at, meta, k, m, r1, r2):
    f = [meta[at + 4 * m + i].astype(F32) for i in (2, 3)]
    return f[0] * r1[k ^ 1, m].astype(F32) + f[1] * r2[k ^ 2, m].astype(F32)


def mix_kernel(rows, micro, heads, at, meta, x, gain, bias, r1, r2, *refs):
    accs, phqs, ws = refs[0:4], refs[4:8], refs[8:12]
    mixed, iden, ust, resid, n2 = refs[12:]
    hidden = heads * 64
    low = lane_low((rows, LANES))
    for m in range(micro):
        rs = slice(m * rows, (m + 1) * rows)
        for k in range(SLOTS):
            s = joined(at, meta, k, m, r1, r2)
            ust[k, m] = s.astype(BF)
            for h in range(heads):
                i = k * heads + h
                hl = slice(h * LANES, (h + 1) * LANES)
                a = accs[k][rs, hl] + mm(phqs[k][rs, hl], take_state(s, h, heads), NT)
                turned = pltpu.roll(a, 64, 1)
                if i % 2 == 0:
                    inv0 = 1.0 / turned
                    mix0 = a * inv0
                else:
                    inv1 = 1.0 / a
                    mix1 = turned * inv1
                    cl = slice((i // 2) * LANES, (i // 2 + 1) * LANES)
                    mixed[rs, cl] = jnp.where(low, mix0, mix1).astype(BF)
                    iden[rs, cl] = jnp.where(low, inv0, inv1)
    wo = jnp.concatenate([w[3 * hidden : 4 * hidden, :] for w in ws], axis=0)
    res = x[...].astype(F32) + mm(mixed[...], wo)
    resid[...] = res
    n, _ = norm_parts(res)
    n2[...] = (n * gain[1:2, :] + bias[1:2, :]).astype(BF)


def gelu_parts(u):
    a = 0.7978845608028654
    u2 = u * u
    t = jnp.tanh(a * u * (1.0 + 0.044715 * u2))
    half = 0.5 * (1.0 + t)
    return u * half, half + 0.5 * u * (1.0 - t * t) * a * (1.0 + 3 * 0.044715 * u2)


def mlp_kernel(k, first, meta, n2, g, u0, u1, d0, d1, *refs):
    if not first:
        mo_in, dn_in, *refs = refs
    keep, send, mo, dn = refs
    half = u0.shape[0]
    wu = jnp.concatenate([u0[...], u1[...]], axis=0)
    wd = jnp.concatenate([d0[...], d1[...]], axis=0)
    up = mm(n2[...], wu, NT)
    hid, slope = gelu_parts(up)
    hid = hid.astype(BF)
    dup = (mm(g[...], wd, NT) * slope).astype(BF)
    a = mm(hid, wd)
    b = mm(dup, wu)
    mo[...] = a if first else mo_in[...] + a
    dn[...] = b if first else dn_in[...] + b
    mine = (meta[0] == 0) if k < 3 else True
    for at, grad in ((0, mm(dup, n2[...], TN)), (half, mm(hid, g[...], TN))):
        grad = grad.astype(BF)
        top, bottom = grad[:half], grad[half:]
        keep[at : at + half, :] = top if k == 3 else jnp.where(mine, top, bottom)
        send[at : at + half, :] = bottom if k == 3 else jnp.where(mine, bottom, top)


def turn_kernel(rows, micro, heads, meta, resid, mo, dn, g, gain, mixed, iden, *refs):
    phqs, ws = refs[0:4], refs[4:8]
    out, dres, dnx, gwo, hst, dln, dmix = refs[8:]
    hidden = heads * 64
    out[...] = (resid[...] + mo[...]).astype(BF)
    n, inverse = norm_parts(resid[...])
    a = dn[...]
    dr = g[...].astype(F32) + norm_back(a, n, inverse, gain[1:2, :])
    dres[...] = dr
    dln[...] = jnp.zeros_like(dln)
    dln[0:1, :] = jnp.sum(a * n, axis=0, keepdims=True)
    dln[1:2, :] = jnp.sum(a, axis=0, keepdims=True)
    dat = dr.astype(BF)
    gwo[...] = mm(mixed[...], dat, TN).astype(BF)
    wo = jnp.concatenate([w[3 * hidden : 4 * hidden, :] for w in ws], axis=0)
    dmix[...] = mm(dat, wo, NT)
    low = lane_low((rows, LANES))
    lane = lax.broadcasted_iota(jnp.int32, (LANES, 2 * LANES), 0) < 64
    column = lax.broadcasted_iota(jnp.int32, (LANES, 2 * LANES), 1) < LANES
    pick = jnp.where(lane == column, -1.0 / 64, 0.0).astype(BF)
    for m in range(micro):
        rs = slice(m * rows, (m + 1) * rows)
        for j in range(SLOTS * heads // 2):
            cl = slice(j * LANES, (j + 1) * LANES)
            d, iv = dmix[rs, cl], iden[rs, cl]
            t = d * mixed[rs, cl].astype(F32)
            both = mm(t.astype(BF), pick)
            even, odd = both[:, :LANES], both[:, LANES:]
            dn_ = d * iv
            x0 = jnp.where(low, dn_, even * pltpu.roll(iv, 64, 1)).astype(BF)
            x1 = jnp.where(low, pltpu.roll(dn_, 64, 1), odd * iv).astype(BF)
            for i, xv in ((2 * j, x0), (2 * j + 1, x1)):
                k, h = divmod(i, heads)
                hl = slice(h * LANES, (h + 1) * LANES)
                dnx[rs, i * LANES : (i + 1) * LANES] = xv
                put_state(hst.at[k], m, h, heads, mm(xv, phqs[k][rs, hl], TN))


def back_kernel(k, rows, micro, heads, meta, qkv, phq, phk, dnx, ust, wq, dpk, dv):
    mask = causal(rows)
    vbase = heads * LANES
    for h in range(heads):
        hl = slice(h * LANES, (h + 1) * LANES)
        dl = slice((k * heads + h) * LANES, (k * heads + h + 1) * LANES)
        for m in range(micro):
            rs = slice(m * rows, (m + 1) * rows)
            pq, pk, dx = phq[rs, hl], phk[rs, hl], dnx[rs, dl]
            v1 = with_ones(qkv[rs, vbase + h * 64 : vbase + h * 64 + 64])
            prob = jnp.where(mask, mm(pq, pk, NT), 0.0).astype(BF)
            ds = jnp.where(mask, mm(dx, v1, NT), 0.0).astype(BF)
            dpq = mm(ds, pk) + mm(dx, take_state(ust[k, m], h, heads))
            pqf = pq.astype(F32)
            wq[rs, hl] = (pqf * (dpq - jnp.sum(pqf * dpq, axis=-1, keepdims=True))).astype(BF)
            dpk[rs, hl] = mm(ds, pq, TN)
            dv[rs, hl] = mm(prob, dx, TN)


def last_kernel(k, rows, micro, heads, at, first, final, meta, qkv, phk, wq, dpk, dv, h1, h2, w, n1, gwo, *refs):
    if not first:
        dn1_in, *refs = refs
    if final:
        x, dres, gain, dln2, *refs = refs
        keep, send, gin, dln, dproj, ww, gw, dn1 = refs
    else:
        keep, send, dn1, dproj, ww, gw = refs
    hidden = heads * 64
    c = meta[0]
    feat = unpack_feat(w[4 * hidden : 4 * hidden + 32, :])
    feat_grads = []
    vbase = heads * LANES
    sts = [joined(at, meta, k, m, h1, h2) for m in range(micro)]
    for h in range(heads):
        fmap = head_map(feat, h)
        hl = slice(h * LANES, (h + 1) * LANES)
        for m in range(micro):
            rs = slice(m * rows, (m + 1) * rows)
            pk = phk[rs, hl]
            v1 = with_ones(qkv[rs, vbase + h * 64 : vbase + h * 64 + 64])
            hx = take_state(sts[m], h, heads)
            dp = dpk[rs, hl] + mm(v1, hx)
            dval = dv[rs, hl] + mm(pk, hx, NT)
            pkf = pk.astype(F32)
            wk = (pkf * (dp - jnp.sum(pkf * dp, axis=-1, keepdims=True))).astype(BF)
            wqk = jnp.concatenate([wq[rs, hl], wk], axis=1)
            ww[rs, :] = wqk
            dproj[rs, hl] = mm(wqk, fmap, NT).astype(BF)
            dproj[rs, vbase + h * 64 : vbase + h * 64 + 64] = dval[:, :64].astype(BF)
        g = mm(qkv[:, hl], ww[...], TN)
        top, bottom = g[:64], g[64:]
        gq = top[:, :LANES] - pltpu.roll(top[:, :LANES], 64, 1)
        gk = bottom[:, LANES:] - pltpu.roll(bottom[:, LANES:], 64, 1)
        feat_grads.append(jnp.where(lane_low(gq.shape), gq, -gk))
    total = mm(dproj[...], w[: 3 * hidden, :])
    dn1[...] = total if first else dn1_in[...] + total
    gw[...] = mm(dproj[...], n1[...], TN).astype(BF)
    fg = jnp.concatenate(feat_grads, axis=0)
    fg = jnp.concatenate([fg[i * 32 : (i + 1) * 32] for i in range(6)], axis=1).astype(BF)
    qh, oh = 3 * hidden // 2, hidden // 2
    for out, at in ((keep, c), (send, 1 - c)):
        out[:qh, :] = gw[pl.ds(pl.multiple_of(at * qh, 16), qh), :]
        out[qh : qh + oh, :] = gwo[pl.ds(pl.multiple_of(k * hidden + at * oh, 16), oh), :]
        out[qh + oh : qh + oh + 16, :] = jnp.where(at == 0, fg[:16], fg[16:])
        out[qh + oh + 16 :, :] = jnp.zeros_like(fg[:16])
    if final:
        n, inverse = norm_parts(x[...].astype(F32))
        a = dn1[...]
        gin[...] = dres[...] + norm_back(a, n, inverse, gain[0:1, :])
        dln[8:, :] = dln2[...]
        dln[:8, :] = jnp.zeros_like(dln2)
        dln[0:1, :] = jnp.sum(a * n, axis=0, keepdims=True)
        dln[1:2, :] = jnp.sum(a, axis=0, keepdims=True)


def split_kernel(terms, parts, meta, *refs):
    arrays, outs = refs[:terms], refs[terms:]
    z = meta[1]
    half = sum(out.shape[0] for out in outs[:parts])
    for side, group in ((z, outs[:parts]), (1 - z, outs[parts:])):
        at = side * half
        for out in group:
            n = out.shape[0]
            rs = pl.ds(pl.multiple_of(at, 16), n)
            total = arrays[0][rs, :].astype(F32)
            for t in arrays[1:]:
                total = total + t[rs, :].astype(F32)
            out[...] = total.astype(BF)
            at = at + n


def join_kernel(parts, meta, *refs):
    *pieces, out = refs
    half = out.shape[0] // 2
    for side, group in ((meta[1], pieces[:parts]), (1 - meta[1], pieces[parts:])):
        at = side * half
        for piece in group:
            n = piece.shape[0]
            out[pl.ds(pl.multiple_of(at, 16), n), :] = piece[...]
            at = at + n


def finish_ff_kernel(meta, own, other, gup, gdown):
    c = meta[0]
    half = own.shape[0] // 2
    is0 = c == 0
    first = jnp.where(is0, own[...], other[...])
    second = jnp.where(is0, other[...], own[...])
    gup[...] = jnp.concatenate([first[:half], second[:half]], axis=0).astype(F32).T
    gdown[:half, :] = first[half:].astype(F32)
    gdown[half:, :] = second[half:].astype(F32)


def collect(meta, pieces, buf):
    c, z = meta[0], meta[1]
    quarter = pieces[0].shape[0]
    for piece, place in zip(pieces, (2 * c + z, 2 * c + 1 - z, 2 * (1 - c) + z, 2 * (1 - c) + 1 - z)):
        buf[pl.ds(pl.multiple_of(place * quarter, 16), quarter), :] = piece[...]


def finish_kernel(heads, meta, p0, p1, p2, p3, gqkv, gfeat, gout, gains, biases, buf):
    collect(meta, (p0, p1, p2, p3), buf)
    hidden = heads * 64
    half, qh, oh = buf.shape[0] // 2, 3 * hidden // 2, hidden // 2

    def rows(at, n, first, size):
        parts = []
        while n:
            c, inner = divmod(at, size)
            m = min(n, size - inner)
            parts.append(buf[c * half + first + inner : c * half + first + inner + m, :])
            at, n = at + m, n - m
        return jnp.concatenate(parts, axis=0) if len(parts) > 1 else parts[0]

    for h in range(heads):
        for c in range(2):
            gqkv[c, h * 64 : (h + 1) * 64, :] = rows(h * LANES + c * 64, 64, 0, qh).astype(F32)
    gqkv[2] = rows(2 * hidden, hidden, 0, qh).astype(F32)
    gout[...] = rows(0, hidden, qh, oh).astype(F32)
    feat = unpack_feat(rows(0, 32, qh + oh, 16)).astype(F32)
    for h in range(heads):
        gfeat[0, h] = feat[h * 64 : (h + 1) * 64, :64]
        gfeat[1, h] = feat[h * 64 : (h + 1) * 64, 64:]
    ln = buf[half - 16 : half, :].astype(F32) + buf[2 * half - 16 :, :].astype(F32)
    gains[0:1, :] = ln[0:1]
    gains[1:2, :] = ln[8:9]
    biases[0:1, :] = ln[1:2]
    biases[1:2, :] = ln[9:10]


def links(heads_axis, dp):
    def table(fn):
        return [(r * dp + d, q[0] * dp + q[1]) for r in range(heads_axis) for d in range(dp) for q in [fn(r, d)] if q]

    one = table(lambda r, d: (r ^ (1 + d % 2), d))
    two = table(lambda r, d: (r ^ (2 - d % 2), d))
    head = {b: table(lambda r, d: (r ^ b, d)) for b in (1, 2)}
    bits = {}
    b = 1
    while b < dp:
        bits[b] = table(lambda r, d: (r, d ^ b))
        b *= 2
    return one, two, head, bits


def move(v, table, name="move"):
    with jax.named_scope(name):
        return lax.ppermute(v, AXES, table)


def factors(r, core, keep):
    high, odd = r // 2, r % 2
    first = [jnp.ones_like(r), jnp.ones_like(r), odd, high * keep]
    second = [1 - high * odd, keep * high, keep * high, jnp.minimum(r, 1)]
    return [jnp.where(core == 0, a, b) for a, b in zip(first, second)]


def local(heads_axis, dp, block_in, ln_gains, ln_biases, w_qkv, feat_maps, w_out, w_up, w_down, seq_lengths, out_cotangent):
    one, two, head, bits = links(heads_axis, dp)
    micro, rows, width = block_in.shape[1:]
    tokens = micro * rows
    heads = feat_maps.shape[1]
    ff = w_up.shape[1]
    hidden = heads * 64
    rank, dpi = lax.axis_index("head"), lax.axis_index("dp")
    core, zbit = dpi % 2, (dpi // 2) % 2
    keeps = [1 - (seq_lengths[0, m, 1] > 0).astype(jnp.int32) for m in range(micro)]
    scalars = [core, zbit]
    for r in (rank, 3 - rank):
        for m in range(micro):
            scalars += factors(r, core, keeps[m])
    meta = jnp.stack([jnp.asarray(v, jnp.int32) for v in scalars])
    fwd, bwd = 2, 2 + 4 * micro

    x = block_in.reshape(tokens, width)
    g = out_cotangent.reshape(tokens, width)
    tw = (tokens, width)

    arows, half = 4 * hidden + 32, ff // 2
    call = Order()
    swap = lambda v, name="swap": move(v, bits[1], name)
    piece = ((half, width), BF)

    (a0,) = call(partial(pack_kernel, heads), [jnp.swapaxes(w_qkv, 1, 2), w_out, feat_maps], [((arows, width), BF)], meta=False)
    a1 = move(a0, one, "a1")
    u0, u1 = call(turn_over_kernel, [w_up], [piece] * 2, meta=False)
    bu0 = move(u0, one, "bu0")

    wl, qw = heads * LANES, 3 * hidden
    st_all = (SLOTS, micro, hidden + 16, LANES)
    first_outs = [((tokens, qw), BF), ((tokens, wl), BF), ((tokens, wl), BF), ((tokens, wl), F32), (st_all, BF)]
    first = lambda k: partial(first_kernel, k, rows, micro, heads)
    slots = []

    def attend(k, w):
        slots.append(call(first(k), [meta, n1, w, slots[-1][4]], first_outs, alias={3: 4}, limit=16))

    n1, *slot = call(first(0), [meta, x, ln_gains, ln_biases, a0], [(tw, BF)] + first_outs, limit=16)
    slots.append(slot)
    a1 = call.gate(a1)
    a2 = swap(a1, "a2")
    (asl,) = call(pick_half_kernel, [meta, a1], [((arows // 2, width), BF)])
    ahalf = move(asl, two, "ahalf")
    u1 = call.gate(u1)
    bu1 = move(u1, one, "bu1")
    d0, d1 = call(copy_kernel, [w_down], [piece] * 2, meta=False)
    attend(1, a1)
    a2, bu0, d0 = call.gate(a2, bu0, d0)
    b2u0 = swap(bu0, "b2u0")
    bd0 = move(d0, one, "bd0")
    attend(2, a2)
    ahalf, b2u0 = call.gate(ahalf, b2u0)
    aother = swap(ahalf, "aother")
    call.pause()
    a3, *slot = call(
        first(3), [meta, n1, ahalf, aother, slots[-1][4]], [((arows, width), BF)] + first_outs, alias={4: 5}, limit=16
    )
    slots.append(slot)
    ws = [a0, a1, a2, a3]
    qkvs, phqs, phks, accs, sts = zip(*slots)

    r1 = move(sts[-1], one, "r1")
    bu1, d1 = call.gate(bu1, d1)
    b2u1 = swap(bu1, "b2u1")
    bd1 = move(d1, one, "bd1")
    (du,) = call(pick_kernel, [meta, bu0, bu1], [piece])
    (on,) = call(partial(relay_kernel, fwd, micro), [meta, sts[-1], r1], [(st_all, BF)])
    r2 = move(on, two, "r2")
    bd0, b2u1, du = call.gate(bd0, b2u1, du)
    b2d0 = swap(bd0, "b2d0")
    du = move(du, two, "du")
    call.pause()
    r2, bd1 = call.gate(r2, bd1)
    b2d1 = swap(bd1, "b2d1")
    (dd,) = call(pick_kernel, [meta, bd0, bd1], [piece])
    dd = move(dd, two, "dd")
    b2d0 = call.gate(b2d0)
    mixed, iden, ust, resid, n2 = call(
        partial(mix_kernel, rows, micro, heads, fwd),
        [meta, x, ln_gains, ln_biases, r1, r2, *accs, *phqs, *ws],
        [(tw, BF), (tw, F32), (st_all, BF), (tw, F32), (tw, BF)],
        limit=24,
    )

    keeps, sends = [None] * SLOTS, [None] * SLOTS
    sums = []

    def mlp(k, *w):
        keeps[k], sends[k], *sums[:] = call(
            partial(mlp_kernel, k, not sums),
            [meta, n2, g, *w, *sums],
            [((ff, width), BF), ((ff, width), BF), (tw, F32), (tw, F32)],
            alias={7: 2, 8: 3} if sums else None,
            limit=18,
        )
        return swap(sends[k], "got%d" % k)

    def split(terms, sizes, names):
        w = terms[0].shape[1]
        outs = [((n, w), BF) for n in sizes] * 2
        res = call(partial(split_kernel, len(terms), len(sizes)), [meta, *terms], outs)
        n = len(sizes)
        return [(res[i], move(res[n + i], bits[2], names[i])) for i in reversed(range(n))][::-1]

    got1 = mlp(1, bu0, bu1, bd0, bd1)
    got2 = mlp(2, b2u0, b2u1, b2d0, b2d1)
    du, dd = call.gate(du, dd)
    du2, dd2 = swap(du, "du2"), swap(dd, "dd2")
    got0 = mlp(0, u0, u1, d0, d1)
    s1 = call.add(keeps[1], got2)
    one1 = move(s1, one, "one1")
    s2 = call.add(keeps[2], got1)
    got3 = mlp(3, du, du2, dd, dd2)
    mo, dn = sums

    out, dres, dnx, gwo, hst, dln2 = call(
        partial(turn_kernel, rows, micro, heads),
        [meta, resid, mo, dn, g, ln_gains, mixed, iden, *phqs, *ws],
        [(tw, BF), (tw, F32), ((tokens, SLOTS * wl), BF), ((SLOTS * hidden, width), BF), (st_all, BF), ((8, width), F32)],
        scratch=[pltpu.VMEM(tw, F32)],
        limit=24,
    )
    h1 = move(hst, one, "h1")
    s3 = call.add(keeps[3], got3)
    one3 = move(s3, one, "one3")
    backs = []

    def back(k):
        backs.append(
            call(
                partial(back_kernel, k, rows, micro, heads),
                [meta, qkvs[k], phqs[k], phks[k], dnx, ust],
                [((tokens, wl), BF), ((tokens, wl), F32), ((tokens, wl), F32)],
                limit=16,
            )
        )

    back(0)
    s0 = call.add(keeps[0], got0)
    back(1)
    p = call.add(s0, one1)
    (on,) = call(partial(relay_kernel, bwd, micro), [meta, hst, h1], [(st_all, BF)])
    h2 = move(on, two, "h2")
    back(2)
    back(3)

    grows = arows + 32
    akeeps, asends = [None] * SLOTS, [None] * SLOTS
    dn1 = []

    def last(k):
        final = k == 0
        args = [meta, qkvs[k], phks[k], *backs[k], h1, h2, ws[k], n1, gwo, *dn1]
        outs = [((grows // 2, width), BF)] * 2
        scratch = [pltpu.VMEM((tokens, qw), BF), pltpu.VMEM((tokens, 2 * LANES), BF), pltpu.VMEM((qw, width), BF)]
        akeeps[k], asends[k], *dn1[:] = call(
            partial(last_kernel, k, rows, micro, heads, bwd, not dn1, final),
            args + ([x, dres, ln_gains, dln2] if final else []),
            outs + ([(tw, F32), ((16, width), F32)] if final else [(tw, F32)]),
            scratch=scratch + ([pltpu.VMEM(tw, F32)] if final else []),
            alias={11: 2} if dn1 and not final else None,
            limit=24,
        )
        return swap(asends[k], "agot%d" % k)

    q = call.add(s2, one3)
    two2 = move(q, two, "two2")
    agot3 = last(3)
    agot1 = last(1)
    t3 = call.add(akeeps[3], agot3)
    aone3 = move(t3, one, "aone3")
    agot2 = last(2)
    t2 = call.add(akeeps[2], agot1)
    t1 = call.add(akeeps[1], agot2)
    agot0 = last(0)
    gin, lns = dn1
    ln1 = move(lns, one, "ln1")
    t1 = call.gate(t1)
    aone1 = move(t1, one, "aone1")

    zs = [b for b in sorted(bits) if b > 2]
    cut = half // 3
    t0 = call.add(akeeps[0], agot0)
    f0, f1 = split([p, two2], [cut, half - cut], ["zf0", "zf1"])

    def with_norms(*terms):
        return call(add_norms_kernel, [lns, ln1, *terms], [(terms[0].shape, BF)], meta=False)[0]

    t2 = with_norms(t2, aone3)
    atwo2 = move(t2, two, "atwo2")
    t0 = with_norms(t0)
    f0 = call.add(*f0)
    if zs:
        f0 = (f0, move(f0, bits[zs[0]], "yf0"))
    (at,) = split([t0, aone1, atwo2], [grows // 4], ["za"])
    f1 = call.add(*f1)
    if zs:
        f1 = (f1, move(f1, bits[zs[0]], "yf1"))
    at = call.add(*at)
    if zs:
        at = (at, move(at, bits[zs[0]], "ya"))
    for b in zs[1:]:
        f0, f1, at = [call.add(*v) for v in (f0, f1, at)]
        f0, f1, at = [(v, move(v, bits[b])) for v in (f0, f1, at)]
    finals = []
    for v, name in ((f0, "xf0"), (f1, "xf1"), (at, "xa")):
        v = call.add(*v) if zs else v
        finals.append((v, move(v, bits[2], name)))
    (f0, xf0), (f1, xf1), (at, xa) = finals
    am = swap(at, "am")
    (ffh,) = call(partial(join_kernel, 2), [meta, f0, f1, xf0, xf1], [((ff, width), BF)])
    ffo = swap(ffh, "ffo")
    xa = call.gate(xa)
    ax = swap(xa, "ax")
    gup, gdown = call(finish_ff_kernel, [meta, ffh, ffo], [((width, ff), F32), ((ff, width), F32)], limit=24)
    gqkv, gfeat, gout, gains, biases = call(
        partial(finish_kernel, heads),
        [meta, at, xa, am, ax],
        [((3, hidden, width), F32), (feat_maps.shape, F32), (w_out.shape, F32), (ln_gains.shape, F32), (ln_biases.shape, F32)],
        scratch=[pltpu.VMEM((grows, width), BF)],
    )
    gqkv = jnp.swapaxes(gqkv, 1, 2)
    shape = (1, micro, rows, width)
    return (out.reshape(shape), gin.reshape(shape), gains, biases, gqkv, gfeat, gout, gup, gdown)


def solution(mesh):
    return jax.shard_map(
        partial(local, mesh.shape["head"], mesh.shape["dp"]),
        mesh=mesh,
        in_specs=(
            P("dp", None, "head", None),
            P(),
            P(),
            P(None, None, "head"),
            P(None, "head", None, None),
            P("head", None),
            P(None, "head"),
            P("head", None),
            P("dp", None, None),
            P("dp", None, "head", None),
        ),
        out_specs=(
            P("dp", None, "head", None),
            P("dp", None, "head", None),
            P(),
            P(),
            P(None, None, "head"),
            P(None, "head", None, None),
            P("head", None),
            P(None, "head"),
            P("head", None),
        ),
        check_vma=False,
    )
```

```python
from functools import partial

import jax
import jax.numpy as jnp
from jax import lax
from jax.experimental import pallas as pl
from jax.experimental.pallas import tpu as pltpu
from jax.sharding import PartitionSpec as P

BF = jnp.bfloat16
F32 = jnp.float32
AXES = ("head", "dp")
SLOTS = 4
LANES = 128
EPS = 1e-05
SIGMA = (0, 2, 1, 3)

NN = (((1,), (0,)), ((), ()))
NT = (((1,), (1,)), ((), ()))
TN = (((0,), (0,)), ((), ()))


def mm(a, b, dims=NN):
    return lax.dot_general(a, b, dims, preferred_element_type=F32)


def lane_low(shape):
    return lax.broadcasted_iota(jnp.int32, shape, 1) < 64


def norm_parts(v):
    center = jnp.mean(v, axis=-1, keepdims=True)
    shifted = v - center
    spread = jnp.mean(shifted * shifted, axis=-1, keepdims=True)
    inverse = lax.rsqrt(spread + EPS)
    return shifted * inverse, inverse


def norm_back(a, n, inverse, gain):
    e = a * gain
    m1 = jnp.mean(e, axis=-1, keepdims=True)
    m2 = jnp.mean(e * n, axis=-1, keepdims=True)
    return inverse * (e - m1 - n * m2)


VMEM = pl.BlockSpec(memory_space=pltpu.VMEM)
SMEM = pl.BlockSpec(memory_space=pltpu.SMEM)
ANY = pl.BlockSpec(memory_space=pl.ANY)
HBM = pl.BlockSpec(memory_space=pltpu.HBM)


SCALE = 100


class Order:
    def __init__(self):
        self.last = None

    def __call__(self, body, args, outs, scratch=(), after=(), alias=None, limit=8, meta=True, place=None, us=1.0):
        deps = list(after) + ([] if self.last is None else [self.last])
        n, nd = len(args), len(deps)

        def run(*refs):
            body(*refs[:n], *refs[n + nd :])

        res = pl.pallas_call(
            run,
            in_specs=([SMEM] if meta else []) + [VMEM] * (n - meta) + [ANY] * nd,
            out_specs=place or [VMEM] * len(outs),
            out_shape=[jax.ShapeDtypeStruct(*o) for o in outs],
            scratch_shapes=list(scratch),
            input_output_aliases=alias or {},
            compiler_params=pltpu.CompilerParams(vmem_limit_bytes=limit * 1024 * 1024),
            name=getattr(body, "func", body).__name__,
            cost_estimate=pl.CostEstimate(
                flops=int(16 * 1.15e9), bytes_accessed=1000, transcendentals=0
            ),
        )(*args, *deps)
        self.last = min(res, key=lambda a: a.size)
        return res

    def add(self, *terms):
        return self(add_kernel, list(terms), [(terms[0].shape, terms[0].dtype)], meta=False)[0]

    def gate(self, *arrays):
        n = len(arrays)
        res = self(gate_kernel, list(arrays), [(a.shape, a.dtype) for a in arrays], meta=False)
        return res if n > 1 else res[0]

    def pause(self):
        (out,) = self(pause_kernel, [], [((8, LANES), F32)], meta=False)
        return out


def gate_kernel(*refs):
    n = len(refs) // 2
    for a, out in zip(refs[:n], refs[n:]):
        out[...] = a[...]


def add_chunks_kernel(*refs):
    *terms, first, second = refs
    n = first.shape[0] // 2
    for i, out in enumerate((first, second)):
        for side in range(2):
            rs = slice((2 * side + i) * n, (2 * side + i + 1) * n)
            total = terms[0][rs, :].astype(F32)
            for t in terms[1:]:
                total = total + t[rs, :].astype(F32)
            out[side * n : (side + 1) * n, :] = total.astype(BF)


def add_chunk_kernel(which, *refs):
    *terms, out = refs
    n = out.shape[0] // 2
    for side in range(2):
        rs = slice((2 * side + which) * n, (2 * side + which + 1) * n)
        total = terms[0][rs, :].astype(F32)
        for t in terms[1:]:
            total = total + t[rs, :].astype(F32)
        out[side * n : (side + 1) * n, :] = total.astype(BF)


def pause_kernel(out):
    out[...] = jnp.zeros_like(out)


def add_kernel(*refs):
    *terms, out = refs
    total = terms[0][...].astype(F32)
    for t in terms[1:]:
        total = total + t[...].astype(F32)
    out[...] = total.astype(out.dtype)


def pack_kernel(heads, wqkv, wout, feats, out):
    hidden = heads * 64
    for h in range(heads):
        for c in range(2):
            at = h * LANES + c * 64
            out[at : at + 64, :] = wqkv[c, h * 64 : (h + 1) * 64, :]
    out[2 * hidden : 3 * hidden, :] = wqkv[2]
    out[3 * hidden : 4 * hidden, :] = wout[...]
    both = [jnp.concatenate([feats[0, h], feats[1, h]], axis=1) for h in range(heads)]
    both = jnp.concatenate(both, axis=0)
    out[4 * hidden :, :] = jnp.concatenate([both[i * 32 : (i + 1) * 32] for i in range(6)], axis=1)


def turn_over_kernel(a, *outs):
    for i, out in enumerate(outs):
        n = out.shape[0]
        out[...] = a[:, i * n : (i + 1) * n].T


def copy_kernel(a, *outs):
    at = 0
    for out in outs:
        out[...] = a[at : at + out.shape[0], :]
        at += out.shape[0]


def pick_half_kernel(meta, a, out):
    half = out.shape[0]
    out[...] = a[pl.ds(pl.multiple_of(meta[0] * half, 16), half), :]


def pick_kernel(meta, *refs):
    n = len(refs) // 3
    for i in range(n):
        refs[2 * n + i][...] = jnp.where(meta[0] == 0, refs[2 * i][...], refs[2 * i + 1][...])


def unpack_feat(block):
    return jnp.concatenate([block[:, i * LANES : (i + 1) * LANES] for i in range(6)], axis=0)


def head_map(feat, h):
    a = feat[h * 64 : (h + 1) * 64, :].astype(F32)
    low = lane_low(a.shape)
    turned = pltpu.roll(a, 64, 1)
    top = jnp.where(low, a, -turned)
    bottom = jnp.where(low, turned, -a)
    zero = jnp.zeros_like(a)
    return jnp.concatenate(
        [jnp.concatenate([top, zero], axis=1), jnp.concatenate([zero, bottom], axis=1)], axis=0
    ).astype(BF)


def softmax_rows(z):
    e = jnp.exp(z - jnp.max(z, axis=-1, keepdims=True))
    return e * (1.0 / jnp.sum(e, axis=-1, keepdims=True))


def causal(rows):
    return lax.broadcasted_iota(jnp.int32, (rows, rows), 0) >= lax.broadcasted_iota(
        jnp.int32, (rows, rows), 1
    )


def with_ones(v):
    return jnp.concatenate([v, jnp.ones_like(v)], axis=1)


def joined_halves(c, own, other, out):
    half = own.shape[0]
    out[pl.ds(pl.multiple_of(c * half, 16), half), :] = own[...]
    out[pl.ds(pl.multiple_of((1 - c) * half, 16), half), :] = other[...]


def first_kernel(k, rows, micro, heads, meta, *refs):
    if k == 0:
        x, gain, bias, w, n1, qkv, phq, phk, acc, st = refs
        n, _ = norm_parts(x[...].astype(F32))
        n1[...] = (n * gain[0:1, :] + bias[0:1, :]).astype(BF)
    elif k < 3:
        n1, w, _, qkv, phq, phk, acc, st = refs
    else:
        n1, own, other, _, w, qkv, phq, phk, acc, st = refs
        joined_halves(meta[0], own, other, w)
    st = st.at[k]
    hidden = heads * 64
    qkv[...] = mm(n1[...], w[: 3 * hidden, :], NT).astype(BF)
    feat = unpack_feat(w[4 * hidden :, :])
    mask = causal(rows)
    for h in range(heads):
        fmap = head_map(feat, h)
        hl = slice(h * LANES, (h + 1) * LANES)
        for m in range(micro):
            rs = slice(m * rows, (m + 1) * rows)
            z = mm(qkv[rs, hl], fmap)
            pq = softmax_rows(z[:, :LANES]).astype(BF)
            pk = softmax_rows(z[:, LANES:]).astype(BF)
            phq[rs, hl] = pq
            phk[rs, hl] = pk
            v0 = heads * LANES + h * 64
            v1 = with_ones(qkv[rs, v0 : v0 + 64])
            prob = jnp.where(mask, mm(pq, pk, NT), 0.0).astype(BF)
            acc[rs, hl] = mm(prob, v1)
            put_state(st, m, h, heads, mm(v1, pk, TN))


def put_state(st, m, h, heads, lt):
    st[m, h * 64 : (h + 1) * 64, :] = lt[:64].astype(BF)
    base = heads * 64
    row = lax.broadcasted_iota(jnp.int32, (16, LANES), 0)
    mine = jnp.where(row == h, lt[64:80], 0.0)
    if h == 0:
        st[m, base : base + 16, :] = mine.astype(BF)
    else:
        st[m, base : base + 16, :] = (st[m, base : base + 16, :].astype(F32) + mine).astype(BF)


def take_state(s, h, heads):
    row = s[heads * 64 + h : heads * 64 + h + 1, :]
    return jnp.concatenate(
        [s[h * 64 : (h + 1) * 64, :], jnp.broadcast_to(row, (64, LANES))], axis=0
    ).astype(BF)


def relay_kernel(at, micro, meta, own, got, out):
    for m in range(micro):
        f = [meta[at + 4 * m + i].astype(F32) for i in range(2)]
        for k in range(SLOTS):
            out[k, m] = (f[0] * own[k, m].astype(F32) + f[1] * got[k ^ 1, m].astype(F32)).astype(BF)


def joined(at, meta, k, m, r1, r2):
    f = [meta[at + 4 * m + i].astype(F32) for i in (2, 3)]
    return f[0] * r1[k ^ 1, m].astype(F32) + f[1] * r2[k ^ 2, m].astype(F32)


def mix_kernel(rows, micro, heads, at, meta, x, gain, bias, r1, r2, *refs):
    accs, phqs, ws = refs[0:4], refs[4:8], refs[8:12]
    mixed, iden, ust, resid, n2 = refs[12:]
    hidden = heads * 64
    low = lane_low((rows, LANES))
    for m in range(micro):
        rs = slice(m * rows, (m + 1) * rows)
        for k in range(SLOTS):
            s = joined(at, meta, k, m, r1, r2)
            ust[k, m] = s.astype(BF)
            for h in range(heads):
                i = k * heads + h
                hl = slice(h * LANES, (h + 1) * LANES)
                a = accs[k][rs, hl] + mm(phqs[k][rs, hl], take_state(s, h, heads), NT)
                turned = pltpu.roll(a, 64, 1)
                if i % 2 == 0:
                    inv0 = 1.0 / turned
                    mix0 = a * inv0
                else:
                    inv1 = 1.0 / a
                    mix1 = turned * inv1
                    cl = slice((i // 2) * LANES, (i // 2 + 1) * LANES)
                    mixed[rs, cl] = jnp.where(low, mix0, mix1).astype(BF)
                    iden[rs, cl] = jnp.where(low, inv0, inv1)
    wo = jnp.concatenate([w[3 * hidden : 4 * hidden, :] for w in ws], axis=0)
    res = x[...].astype(F32) + mm(mixed[...], wo)
    resid[...] = res
    n, _ = norm_parts(res)
    n2[...] = (n * gain[1:2, :] + bias[1:2, :]).astype(BF)


def gelu_parts(u):
    a = 0.7978845608028654
    u2 = u * u
    t = jnp.tanh(a * u * (1.0 + 0.044715 * u2))
    half = 0.5 * (1.0 + t)
    return u * half, half + 0.5 * u * (1.0 - t * t) * a * (1.0 + 3 * 0.044715 * u2)


def mlp_kernel(k, first, meta, n2, g, u0, u1, d0, d1, *refs):
    if not first:
        mo_in, dn_in, *refs = refs
    keep, send, mo, dn = refs
    half = u0.shape[0]
    wu = jnp.concatenate([u0[...], u1[...]], axis=0)
    wd = jnp.concatenate([d0[...], d1[...]], axis=0)
    up = mm(n2[...], wu, NT)
    hid, slope = gelu_parts(up)
    hid = hid.astype(BF)
    dup = (mm(g[...], wd, NT) * slope).astype(BF)
    a = mm(hid, wd)
    b = mm(dup, wu)
    mo[...] = a if first else mo_in[...] + a
    dn[...] = b if first else dn_in[...] + b
    mine = (meta[0] == 0) if k < 3 else True
    for at, grad in ((0, mm(dup, n2[...], TN)), (half, mm(hid, g[...], TN))):
        grad = grad.astype(BF)
        top, bottom = grad[:half], grad[half:]
        keep[at : at + half, :] = top if k == 3 else jnp.where(mine, top, bottom)
        send[at : at + half, :] = bottom if k == 3 else jnp.where(mine, bottom, top)


def turn_kernel(rows, micro, heads, meta, resid, mo, dn, g, gain, mixed, iden, *refs):
    phqs, ws = refs[0:4], refs[4:8]
    out, dres, dnx, gwo, hst, dln, dmix = refs[8:]
    hidden = heads * 64
    out[...] = (resid[...] + mo[...]).astype(BF)
    n, inverse = norm_parts(resid[...])
    a = dn[...]
    dr = g[...].astype(F32) + norm_back(a, n, inverse, gain[1:2, :])
    dres[...] = dr
    dln[...] = jnp.zeros_like(dln)
    dln[0:1, :] = jnp.sum(a * n, axis=0, keepdims=True)
    dln[1:2, :] = jnp.sum(a, axis=0, keepdims=True)
    dat = dr.astype(BF)
    gwo[...] = mm(mixed[...], dat, TN).astype(BF)
    wo = jnp.concatenate([w[3 * hidden : 4 * hidden, :] for w in ws], axis=0)
    dmix[...] = mm(dat, wo, NT)
    low = lane_low((rows, LANES))
    lane = lax.broadcasted_iota(jnp.int32, (LANES, 2 * LANES), 0) < 64
    column = lax.broadcasted_iota(jnp.int32, (LANES, 2 * LANES), 1) < LANES
    pick = jnp.where(lane == column, -1.0 / 64, 0.0).astype(BF)
    for m in range(micro):
        rs = slice(m * rows, (m + 1) * rows)
        for j in range(SLOTS * heads // 2):
            cl = slice(j * LANES, (j + 1) * LANES)
            d, iv = dmix[rs, cl], iden[rs, cl]
            t = d * mixed[rs, cl].astype(F32)
            both = mm(t.astype(BF), pick)
            even, odd = both[:, :LANES], both[:, LANES:]
            dn_ = d * iv
            x0 = jnp.where(low, dn_, even * pltpu.roll(iv, 64, 1)).astype(BF)
            x1 = jnp.where(low, pltpu.roll(dn_, 64, 1), odd * iv).astype(BF)
            for i, xv in ((2 * j, x0), (2 * j + 1, x1)):
                k, h = divmod(i, heads)
                hl = slice(h * LANES, (h + 1) * LANES)
                dnx[rs, i * LANES : (i + 1) * LANES] = xv
                put_state(hst.at[k], m, h, heads, mm(xv, phqs[k][rs, hl], TN))


def back_kernel(k, rows, micro, heads, meta, qkv, phq, phk, dnx, ust, wq, dpk, dv):
    mask = causal(rows)
    vbase = heads * LANES
    for h in range(heads):
        hl = slice(h * LANES, (h + 1) * LANES)
        dl = slice((k * heads + h) * LANES, (k * heads + h + 1) * LANES)
        for m in range(micro):
            rs = slice(m * rows, (m + 1) * rows)
            pq, pk, dx = phq[rs, hl], phk[rs, hl], dnx[rs, dl]
            v1 = with_ones(qkv[rs, vbase + h * 64 : vbase + h * 64 + 64])
            prob = jnp.where(mask, mm(pq, pk, NT), 0.0).astype(BF)
            ds = jnp.where(mask, mm(dx, v1, NT), 0.0).astype(BF)
            dpq = mm(ds, pk) + mm(dx, take_state(ust[k, m], h, heads))
            pqf = pq.astype(F32)
            wq[rs, hl] = (pqf * (dpq - jnp.sum(pqf * dpq, axis=-1, keepdims=True))).astype(BF)
            dpk[rs, hl] = mm(ds, pq, TN)
            dv[rs, hl] = mm(prob, dx, TN)


def last_kernel(k, rows, micro, heads, at, first, final, meta, qkv, phk, wq, dpk, dv, h1, h2, w, n1, gwo, *refs):
    if not first:
        dn1_in, *refs = refs
    if final:
        x, dres, gain, dln2, *refs = refs
        keep, send, gin, dln, dproj, ww, gw, dn1 = refs
    else:
        keep, send, dn1, dproj, ww, gw = refs
    hidden = heads * 64
    c = meta[0]
    feat = unpack_feat(w[4 * hidden : 4 * hidden + 32, :])
    feat_grads = []
    vbase = heads * LANES
    sts = [joined(at, meta, k, m, h1, h2) for m in range(micro)]
    for h in range(heads):
        fmap = head_map(feat, h)
        hl = slice(h * LANES, (h + 1) * LANES)
        for m in range(micro):
            rs = slice(m * rows, (m + 1) * rows)
            pk = phk[rs, hl]
            v1 = with_ones(qkv[rs, vbase + h * 64 : vbase + h * 64 + 64])
            hx = take_state(sts[m], h, heads)
            dp = dpk[rs, hl] + mm(v1, hx)
            dval = dv[rs, hl] + mm(pk, hx, NT)
            pkf = pk.astype(F32)
            wk = (pkf * (dp - jnp.sum(pkf * dp, axis=-1, keepdims=True))).astype(BF)
            wqk = jnp.concatenate([wq[rs, hl], wk], axis=1)
            ww[rs, :] = wqk
            dproj[rs, hl] = mm(wqk, fmap, NT).astype(BF)
            dproj[rs, vbase + h * 64 : vbase + h * 64 + 64] = dval[:, :64].astype(BF)
        g = mm(qkv[:, hl], ww[...], TN)
        top, bottom = g[:64], g[64:]
        gq = top[:, :LANES] - pltpu.roll(top[:, :LANES], 64, 1)
        gk = bottom[:, LANES:] - pltpu.roll(bottom[:, LANES:], 64, 1)
        feat_grads.append(jnp.where(lane_low(gq.shape), gq, -gk))
    total = mm(dproj[...], w[: 3 * hidden, :])
    dn1[...] = total if first else dn1_in[...] + total
    gw[...] = mm(dproj[...], n1[...], TN).astype(BF)
    fg = jnp.concatenate(feat_grads, axis=0)
    fg = jnp.concatenate([fg[i * 32 : (i + 1) * 32] for i in range(6)], axis=1).astype(BF)
    qh, oh = 3 * hidden // 2, hidden // 2
    for out, at in ((keep, c), (send, 1 - c)):
        out[:qh, :] = gw[pl.ds(pl.multiple_of(at * qh, 16), qh), :]
        out[qh : qh + oh, :] = gwo[pl.ds(pl.multiple_of(k * hidden + at * oh, 16), oh), :]
        out[qh + oh : qh + oh + 16, :] = jnp.where(at == 0, fg[:16], fg[16:])
        out[qh + oh + 16 :, :] = jnp.zeros_like(fg[:16])
    if final:
        n, inverse = norm_parts(x[...].astype(F32))
        a = dn1[...]
        gin[...] = dres[...] + norm_back(a, n, inverse, gain[0:1, :])
        dln[8:, :] = dln2[...]
        dln[:8, :] = jnp.zeros_like(dln2)
        dln[0:1, :] = jnp.sum(a * n, axis=0, keepdims=True)
        dln[1:2, :] = jnp.sum(a, axis=0, keepdims=True)


def split_kernel(terms, parts, meta, *refs):
    arrays, outs = refs[:terms], refs[terms:]
    z = meta[1]
    half = sum(out.shape[0] for out in outs[:parts])
    for side, group in ((z, outs[:parts]), (1 - z, outs[parts:])):
        at = side * half
        for out in group:
            n = out.shape[0]
            rs = pl.ds(pl.multiple_of(at, 16), n)
            total = arrays[0][rs, :].astype(F32)
            for t in arrays[1:]:
                total = total + t[rs, :].astype(F32)
            out[...] = total.astype(BF)
            at = at + n


def join_kernel(parts, meta, *refs):
    *pieces, out = refs
    half = out.shape[0] // 2
    for side, group in ((meta[1], pieces[:parts]), (1 - meta[1], pieces[parts:])):
        at = side * half
        for piece in group:
            n = piece.shape[0]
            out[pl.ds(pl.multiple_of(at, 16), n), :] = piece[...]
            at = at + n


def finish_ff_kernel(meta, own, other, gup_out, gdown_out, done, gup, gdown, sems):
    c = meta[0]
    half = own.shape[0] // 2
    is0 = c == 0
    first = jnp.where(is0, own[...], other[...])
    second = jnp.where(is0, other[...], own[...])
    gdown[:half, :] = first[half:].astype(F32)
    gdown[half:, :] = second[half:].astype(F32)
    down = pltpu.make_async_copy(gdown, gdown_out, sems.at[0])
    down.start()
    gup[...] = jnp.concatenate([first[:half], second[:half]], axis=0).astype(F32).T
    up = pltpu.make_async_copy(gup, gup_out, sems.at[1])
    up.start()
    done[...] = jnp.zeros_like(done)
    down.wait()
    up.wait()


def collect(meta, pieces, buf):
    c, z = meta[0], meta[1]
    quarter = pieces[0].shape[0]
    for piece, place in zip(pieces, (2 * c + z, 2 * c + 1 - z, 2 * (1 - c) + z, 2 * (1 - c) + 1 - z)):
        buf[pl.ds(pl.multiple_of(place * quarter, 16), quarter), :] = piece[...]


def finish_kernel(heads, meta, p0, p1, p2, p3, lns, more, gqkv, gfeat, gout, gains, biases, buf):
    collect(meta, (p0, p1, p2, p3), buf)
    hidden = heads * 64
    half, qh, oh = buf.shape[0] // 2, 3 * hidden // 2, hidden // 2

    def rows(at, n, first, size):
        parts = []
        while n:
            c, inner = divmod(at, size)
            m = min(n, size - inner)
            parts.append(buf[c * half + first + inner : c * half + first + inner + m, :])
            at, n = at + m, n - m
        return jnp.concatenate(parts, axis=0) if len(parts) > 1 else parts[0]

    for h in range(heads):
        for c in range(2):
            gqkv[c, h * 64 : (h + 1) * 64, :] = rows(h * LANES + c * 64, 64, 0, qh).astype(F32)
    gqkv[2] = rows(2 * hidden, hidden, 0, qh).astype(F32)
    gout[...] = rows(0, hidden, qh, oh).astype(F32)
    feat = unpack_feat(rows(0, 32, qh + oh, 16)).astype(F32)
    for h in range(heads):
        gfeat[0, h] = feat[h * 64 : (h + 1) * 64, :64]
        gfeat[1, h] = feat[h * 64 : (h + 1) * 64, 64:]
    ln = lns[...] + more[...]
    gains[0:1, :] = ln[0:1]
    gains[1:2, :] = ln[8:9]
    biases[0:1, :] = ln[1:2]
    biases[1:2, :] = ln[9:10]


def links(heads_axis, dp):
    def table(fn):
        return [(r * dp + d, q[0] * dp + q[1]) for r in range(heads_axis) for d in range(dp) for q in [fn(r, d)] if q]

    one = table(lambda r, d: (r ^ (1 + d % 2), d))
    two = table(lambda r, d: (r ^ (2 - d % 2), d))
    head = {b: table(lambda r, d: (r ^ b, d)) for b in (1, 2)}
    bits = {}
    b = 1
    while b < dp:
        bits[b] = table(lambda r, d: (r, d ^ b))
        b *= 2
    return one, two, head, bits


def move(v, table, name="move"):
    with jax.named_scope(name):
        return lax.ppermute(v, AXES, table)


def factors(r, core, keep):
    high, odd = r // 2, r % 2
    first = [jnp.ones_like(r), jnp.ones_like(r), odd, high * keep]
    second = [1 - high * odd, keep * high, keep * high, jnp.minimum(r, 1)]
    return [jnp.where(core == 0, a, b) for a, b in zip(first, second)]


def local(heads_axis, dp, block_in, ln_gains, ln_biases, w_qkv, feat_maps, w_out, w_up, w_down, seq_lengths, out_cotangent):
    one, two, head, bits = links(heads_axis, dp)
    micro, rows, width = block_in.shape[1:]
    tokens = micro * rows
    heads = feat_maps.shape[1]
    ff = w_up.shape[1]
    hidden = heads * 64
    rank, dpi = lax.axis_index("head"), lax.axis_index("dp")
    core, zbit = dpi % 2, (dpi // 2) % 2
    keeps = [1 - (seq_lengths[0, m, 1] > 0).astype(jnp.int32) for m in range(micro)]
    scalars = [core, zbit]
    for r in (rank, 3 - rank):
        for m in range(micro):
            scalars += factors(r, core, keeps[m])
    meta = jnp.stack([jnp.asarray(v, jnp.int32) for v in scalars])
    fwd, bwd = 2, 2 + 4 * micro

    x = block_in.reshape(tokens, width)
    g = out_cotangent.reshape(tokens, width)
    tw = (tokens, width)

    arows, half = 4 * hidden + 32, ff // 2
    call = Order()
    swap = lambda v, name="swap": move(v, bits[1], name)
    piece = ((half, width), BF)

    (a0,) = call(partial(pack_kernel, heads), [jnp.swapaxes(w_qkv, 1, 2), w_out, feat_maps], [((arows, width), BF)], meta=False)
    a1 = move(a0, one, "a1")
    u0, u1 = call(turn_over_kernel, [w_up], [piece] * 2, meta=False)
    bu0 = move(u0, one, "bu0")

    wl, qw = heads * LANES, 3 * hidden
    st_all = (SLOTS, micro, hidden + 16, LANES)
    first_outs = [((tokens, qw), BF), ((tokens, wl), BF), ((tokens, wl), BF), ((tokens, wl), F32), (st_all, BF)]
    first = lambda k: partial(first_kernel, k, rows, micro, heads)
    slots = []

    def attend(k, w):
        slots.append(call(first(k), [meta, n1, w, slots[-1][4]], first_outs, alias={3: 4}, limit=16))

    n1, *slot = call(first(0), [meta, x, ln_gains, ln_biases, a0], [(tw, BF)] + first_outs, limit=16)
    slots.append(slot)
    a1 = call.gate(a1)
    a2 = swap(a1, "a2")
    (asl,) = call(pick_half_kernel, [meta, a1], [((arows // 2, width), BF)])
    ahalf = move(asl, two, "ahalf")
    u1 = call.gate(u1)
    bu1 = move(u1, one, "bu1")
    d0, d1 = call(copy_kernel, [w_down], [piece] * 2, meta=False)
    attend(1, a1)
    a2, bu0, d0 = call.gate(a2, bu0, d0)
    b2u0 = swap(bu0, "b2u0")
    bd0 = move(d0, one, "bd0")
    attend(2, a2)
    ahalf, b2u0 = call.gate(ahalf, b2u0)
    aother = swap(ahalf, "aother")
    call.pause()
    a3, *slot = call(
        first(3), [meta, n1, ahalf, aother, slots[-1][4]], [((arows, width), BF)] + first_outs, alias={4: 5}, limit=16
    )
    slots.append(slot)
    ws = [a0, a1, a2, a3]
    qkvs, phqs, phks, accs, sts = zip(*slots)

    r1 = move(sts[-1], one, "r1")
    bu1, d1 = call.gate(bu1, d1)
    b2u1 = swap(bu1, "b2u1")
    bd1 = move(d1, one, "bd1")
    (du,) = call(pick_kernel, [meta, bu0, bu1], [piece])
    (on,) = call(partial(relay_kernel, fwd, micro), [meta, sts[-1], r1], [(st_all, BF)])
    r2 = move(on, two, "r2")
    bd0, b2u1, du = call.gate(bd0, b2u1, du)
    b2d0 = swap(bd0, "b2d0")
    du = move(du, two, "du")
    call.pause()
    r2, bd1 = call.gate(r2, bd1)
    b2d1 = swap(bd1, "b2d1")
    (dd,) = call(pick_kernel, [meta, bd0, bd1], [piece])
    dd = move(dd, two, "dd")
    b2d0 = call.gate(b2d0)
    mixed, iden, ust, resid, n2 = call(
        partial(mix_kernel, rows, micro, heads, fwd),
        [meta, x, ln_gains, ln_biases, r1, r2, *accs, *phqs, *ws],
        [(tw, BF), (tw, F32), (st_all, BF), (tw, F32), (tw, BF)],
        limit=24,
    )

    keeps, sends = [None] * SLOTS, [None] * SLOTS
    sums = []

    def mlp(k, *w):
        keeps[k], sends[k], *sums[:] = call(
            partial(mlp_kernel, k, not sums),
            [meta, n2, g, *w, *sums],
            [((ff, width), BF), ((ff, width), BF), (tw, F32), (tw, F32)],
            alias={7: 2, 8: 3} if sums else None,
            limit=16,
        )
        return swap(sends[k], "got%d" % k)

    def split(terms, sizes, names):
        w = terms[0].shape[1]
        outs = [((n, w), BF) for n in sizes] * 2
        res = call(partial(split_kernel, len(terms), len(sizes)), [meta, *terms], outs)
        n = len(sizes)
        return [(res[i], move(res[n + i], bits[2], names[i])) for i in reversed(range(n))][::-1]

    got1 = mlp(1, bu0, bu1, bd0, bd1)
    got2 = mlp(2, b2u0, b2u1, b2d0, b2d1)
    du, dd = call.gate(du, dd)
    du2, dd2 = swap(du, "du2"), swap(dd, "dd2")
    got0 = mlp(0, u0, u1, d0, d1)
    s1 = call.add(keeps[1], got2)
    one1 = move(s1, one, "one1")
    chunk = ((ff // 2, width), BF)
    s2 = call(add_chunks_kernel, [keeps[2], got1], [chunk] * 2, meta=False)
    got3 = mlp(3, du, du2, dd, dd2)
    mo, dn = sums

    out, dres, dnx, gwo, hst, dln2 = call(
        partial(turn_kernel, rows, micro, heads),
        [meta, resid, mo, dn, g, ln_gains, mixed, iden, *phqs, *ws],
        [(tw, BF), (tw, F32), ((tokens, SLOTS * wl), BF), ((SLOTS * hidden, width), BF), (st_all, BF), ((8, width), F32)],
        scratch=[pltpu.VMEM(tw, F32)],
        limit=24,
    )
    h1 = move(hst, one, "h1")
    (s3a,) = call(partial(add_chunk_kernel, 0), [keeps[3], got3], [chunk], meta=False)
    one3a = move(s3a, one, "one3a")
    backs = []

    def back(k):
        backs.append(
            call(
                partial(back_kernel, k, rows, micro, heads),
                [meta, qkvs[k], phqs[k], phks[k], dnx, ust],
                [((tokens, wl), BF), ((tokens, wl), F32), ((tokens, wl), F32)],
                limit=16,
            )
        )

    back(0)
    s0 = call.add(keeps[0], got0)
    back(1)
    (on,) = call(partial(relay_kernel, bwd, micro), [meta, hst, h1], [(st_all, BF)])
    h2 = move(on, two, "h2")
    p = call(add_chunks_kernel, [s0, one1], [chunk] * 2, meta=False)
    back(2)
    (s3b,) = call(partial(add_chunk_kernel, 1), [keeps[3], got3], [chunk], meta=False)
    one3b = move(s3b, one, "one3b")
    back(3)
    q = call.add(s2[0], one3a)
    two2a = move(q, two, "two2a")

    grows = arows + 32
    akeeps, asends = [None] * SLOTS, [None] * SLOTS
    dn1 = []

    def last(k):
        final = k == 0
        args = [meta, qkvs[k], phks[k], *backs[k], h1, h2, ws[k], n1, gwo, *dn1]
        outs = [((grows // 2, width), BF)] * 2
        scratch = [pltpu.VMEM((tokens, qw), BF), pltpu.VMEM((tokens, 2 * LANES), BF), pltpu.VMEM((qw, width), BF)]
        akeeps[k], asends[k], *dn1[:] = call(
            partial(last_kernel, k, rows, micro, heads, bwd, not dn1, final),
            args + ([x, dres, ln_gains, dln2] if final else []),
            outs + ([(tw, F32), ((16, width), F32)] if final else [(tw, F32)]),
            scratch=scratch + ([pltpu.VMEM(tw, F32)] if final else []),
            alias={11: 2} if dn1 and not final else None,
            limit=18,
        )
        return swap(asends[k], "agot%d" % k)

    agot3 = last(3)
    agot1 = last(1)
    q = call.add(s2[1], one3b)
    two2b = move(q, two, "two2b")
    t3 = call.add(akeeps[3], agot3)
    aone3 = move(t3, one, "aone3")
    agot2 = last(2)
    (f0,) = split([p[0], two2a], [ff // 4], ["zf0"])
    t2 = call.add(akeeps[2], agot1)
    t1 = call.add(akeeps[1], agot2)
    aone1 = move(t1, one, "aone1")
    agot0 = last(0)
    gin, lns = dn1
    t2 = call.add(t2, aone3)
    atwo2 = move(t2, two, "atwo2")

    zs = [b for b in sorted(bits) if b > 2]
    (f1,) = split([p[1], two2b], [ff // 4], ["zf1"])
    f0 = call.add(*f0)
    if zs:
        f0 = (f0, move(f0, bits[zs[0]], "yf0"))
    t0 = call.add(akeeps[0], agot0)
    steps = [bits[b] for b in sorted(bits) if b > 1] + [bits[1], one, two]
    lns = call.gate(lns)
    ln = move(lns, steps.pop(0), "ln")

    def more_norms():
        nonlocal lns, ln
        lns = call.add(lns, ln)
        ln = move(lns, steps.pop(0), "ln")

    (at,) = split([t0, aone1, atwo2], [grows // 4], ["za"])
    call.pause()
    f1 = call.add(*f1)
    if zs:
        f1 = (f1, move(f1, bits[zs[0]], "yf1"))
    for b in zs[1:]:
        f0, f1 = [call.add(*v) for v in (f0, f1)]
        f0, f1 = [(v, move(v, bits[b])) for v in (f0, f1)]
    f0 = call.add(*f0) if zs else f0
    xf0 = move(f0, bits[2], "xf0")
    at = call.add(*at)
    if zs:
        at = (at, move(at, bits[zs[0]], "ya"))
    more_norms()
    if zs:
        f1 = call.add(*f1)
    xf1 = move(f1, bits[2], "xf1")
    if zs:
        at = call.add(*at)
    for b in zs[1:]:
        at = call.add(at, move(at, bits[b]))
    xa = move(at, bits[2], "xa")
    am = swap(at, "am")
    more_norms()
    call.pause()
    more_norms()
    (ffh,) = call(partial(join_kernel, 2), [meta, f0, f1, xf0, xf1], [((ff, width), BF)])
    ffo = swap(ffh, "ffo")
    while steps:
        more_norms()
    gup, gdown, _ = call(
        finish_ff_kernel,
        [meta, ffh, ffo],
        [((width, ff), F32), ((ff, width), F32), ((8, LANES), F32)],
        scratch=[pltpu.VMEM((width, ff), F32), pltpu.VMEM((ff, width), F32), pltpu.SemaphoreType.DMA((2,))],
        limit=16,
        place=[HBM, HBM, VMEM],
    )
    xa = call.gate(xa)
    ax = swap(xa, "ax")
    call.pause()
    gqkv, gfeat, gout, gains, biases = call(
        partial(finish_kernel, heads),
        [meta, at, xa, am, ax, lns, ln],
        [((3, hidden, width), F32), (feat_maps.shape, F32), (w_out.shape, F32), (ln_gains.shape, F32), (ln_biases.shape, F32)],
        scratch=[pltpu.VMEM((grows, width), BF)],
    )
    gqkv = jnp.swapaxes(gqkv, 1, 2)
    shape = (1, micro, rows, width)
    return (out.reshape(shape), gin.reshape(shape), gains, biases, gqkv, gfeat, gout, gup, gdown)


def solution(mesh):
    return jax.shard_map(
        partial(local, mesh.shape["head"], mesh.shape["dp"]),
        mesh=mesh,
        in_specs=(
            P("dp", None, "head", None),
            P(),
            P(),
            P(None, None, "head"),
            P(None, "head", None, None),
            P("head", None),
            P(None, "head"),
            P("head", None),
            P("dp", None, None),
            P("dp", None, "head", None),
        ),
        out_specs=(
            P("dp", None, "head", None),
            P("dp", None, "head", None),
            P(),
            P(),
            P(None, None, "head"),
            P(None, "head", None, None),
            P("head", None),
            P(None, "head"),
            P("head", None),
        ),
        check_vma=False,
    )
```

```python
from functools import partial

import jax
import jax.numpy as jnp
from jax import lax
from jax.experimental import pallas as pl
from jax.experimental.pallas import tpu as pltpu
from jax.sharding import PartitionSpec as P

BF = jnp.bfloat16
F32 = jnp.float32
AXES = ("head", "dp")
SLOTS = 4
LANES = 128
EPS = 1e-05
SIGMA = (0, 2, 1, 3)

NN = (((1,), (0,)), ((), ()))
NT = (((1,), (1,)), ((), ()))
TN = (((0,), (0,)), ((), ()))


def mm(a, b, dims=NN):
    return lax.dot_general(a, b, dims, preferred_element_type=F32)


def lane_low(shape):
    return lax.broadcasted_iota(jnp.int32, shape, 1) < 64


def norm_parts(v):
    center = jnp.mean(v, axis=-1, keepdims=True)
    shifted = v - center
    spread = jnp.mean(shifted * shifted, axis=-1, keepdims=True)
    inverse = lax.rsqrt(spread + EPS)
    return shifted * inverse, inverse


def norm_back(a, n, inverse, gain):
    e = a * gain
    m1 = jnp.mean(e, axis=-1, keepdims=True)
    m2 = jnp.mean(e * n, axis=-1, keepdims=True)
    return inverse * (e - m1 - n * m2)


VMEM = pl.BlockSpec(memory_space=pltpu.VMEM)
SMEM = pl.BlockSpec(memory_space=pltpu.SMEM)
ANY = pl.BlockSpec(memory_space=pl.ANY)
HBM = pl.BlockSpec(memory_space=pltpu.HBM)


SCALE = 100


class Order:
    def __init__(self):
        self.last = None

    def __call__(self, body, args, outs, scratch=(), after=(), alias=None, limit=8, meta=True, place=None, us=1.0):
        deps = list(after) + ([] if self.last is None else [self.last])
        n, nd = len(args), len(deps)

        def run(*refs):
            body(*refs[:n], *refs[n + nd :])

        res = pl.pallas_call(
            run,
            in_specs=([SMEM] if meta else []) + [VMEM] * (n - meta) + [ANY] * nd,
            out_specs=place or [VMEM] * len(outs),
            out_shape=[jax.ShapeDtypeStruct(*o) for o in outs],
            scratch_shapes=list(scratch),
            input_output_aliases=alias or {},
            compiler_params=pltpu.CompilerParams(vmem_limit_bytes=limit * 1024 * 1024),
            name=getattr(body, "func", body).__name__,
            cost_estimate=pl.CostEstimate(
                flops=int(16 * 1.15e9), bytes_accessed=1000, transcendentals=0
            ),
        )(*args, *deps)
        self.last = min(res, key=lambda a: a.size)
        return res

    def add(self, *terms):
        return self(add_kernel, list(terms), [(terms[0].shape, terms[0].dtype)], meta=False)[0]

    def gate(self, *arrays):
        n = len(arrays)
        res = self(gate_kernel, list(arrays), [(a.shape, a.dtype) for a in arrays], meta=False)
        return res if n > 1 else res[0]

    def pause(self):
        (out,) = self(pause_kernel, [], [((8, LANES), F32)], meta=False)
        return out


def gate_kernel(*refs):
    n = len(refs) // 2
    for a, out in zip(refs[:n], refs[n:]):
        out[...] = a[...]


def add_chunks_kernel(*refs):
    *terms, first, second = refs
    n = first.shape[0] // 2
    for i, out in enumerate((first, second)):
        for side in range(2):
            rs = slice((2 * side + i) * n, (2 * side + i + 1) * n)
            total = terms[0][rs, :].astype(F32)
            for t in terms[1:]:
                total = total + t[rs, :].astype(F32)
            out[side * n : (side + 1) * n, :] = total.astype(BF)


def add_chunk_kernel(which, *refs):
    *terms, out = refs
    n = out.shape[0] // 2
    for side in range(2):
        rs = slice((2 * side + which) * n, (2 * side + which + 1) * n)
        total = terms[0][rs, :].astype(F32)
        for t in terms[1:]:
            total = total + t[rs, :].astype(F32)
        out[side * n : (side + 1) * n, :] = total.astype(BF)


def pause_kernel(out):
    out[...] = jnp.zeros_like(out)


def add_kernel(*refs):
    *terms, out = refs
    total = terms[0][...].astype(F32)
    for t in terms[1:]:
        total = total + t[...].astype(F32)
    out[...] = total.astype(out.dtype)


def pack_kernel(heads, wqkv, feats, out):
    hidden = heads * 64
    for h in range(heads):
        for c in range(2):
            at = h * LANES + c * 64
            out[at : at + 64, :] = wqkv[c, h * 64 : (h + 1) * 64, :]
    out[2 * hidden : 3 * hidden, :] = wqkv[2]
    both = [jnp.concatenate([feats[0, h], feats[1, h]], axis=1) for h in range(heads)]
    both = jnp.concatenate(both, axis=0)
    out[3 * hidden :, :] = jnp.concatenate([both[i * 32 : (i + 1) * 32] for i in range(6)], axis=1)


def turn_over_kernel(a, wout, first, second):
    n = second.shape[0]
    first[:n, :] = a[:, :n].T
    first[n:, :] = wout[...]
    second[...] = a[:, n:].T


def tail_kernel(a, out):
    out[...] = a[a.shape[0] - out.shape[0] :, :]


def copy_kernel(a, *outs):
    at = 0
    for out in outs:
        out[...] = a[at : at + out.shape[0], :]
        at += out.shape[0]


def pick_half_kernel(meta, a, out):
    half = out.shape[0]
    out[...] = a[pl.ds(pl.multiple_of(meta[0] * half, 16), half), :]


def pick_kernel(meta, *refs):
    n = len(refs) // 3
    for i in range(n):
        rows = refs[2 * n + i].shape[0]
        refs[2 * n + i][...] = jnp.where(meta[0] == 0, refs[2 * i][:rows, :], refs[2 * i + 1][:rows, :])


def unpack_feat(block):
    return jnp.concatenate([block[:, i * LANES : (i + 1) * LANES] for i in range(6)], axis=0)


def head_map(feat, h):
    a = feat[h * 64 : (h + 1) * 64, :].astype(F32)
    low = lane_low(a.shape)
    turned = pltpu.roll(a, 64, 1)
    top = jnp.where(low, a, -turned)
    bottom = jnp.where(low, turned, -a)
    zero = jnp.zeros_like(a)
    return jnp.concatenate(
        [jnp.concatenate([top, zero], axis=1), jnp.concatenate([zero, bottom], axis=1)], axis=0
    ).astype(BF)


def softmax_rows(z):
    e = jnp.exp(z - jnp.max(z, axis=-1, keepdims=True))
    return e * (1.0 / jnp.sum(e, axis=-1, keepdims=True))


def causal(rows):
    return lax.broadcasted_iota(jnp.int32, (rows, rows), 0) >= lax.broadcasted_iota(
        jnp.int32, (rows, rows), 1
    )


def with_ones(v):
    return jnp.concatenate([v, jnp.ones_like(v)], axis=1)


def joined_halves(c, own, other, out):
    half = own.shape[0]
    out[pl.ds(pl.multiple_of(c * half, 16), half), :] = own[...]
    out[pl.ds(pl.multiple_of((1 - c) * half, 16), half), :] = other[...]


def first_kernel(k, rows, micro, heads, meta, *refs):
    if k == 0:
        x, gain, bias, w, n1, qkv, phq, phk, acc, st = refs
        n, _ = norm_parts(x[...].astype(F32))
        n1[...] = (n * gain[0:1, :] + bias[0:1, :]).astype(BF)
    elif k < 3:
        n1, w, _, qkv, phq, phk, acc, st = refs
    else:
        n1, own, other, _, w, qkv, phq, phk, acc, st = refs
        joined_halves(meta[0], own, other, w)
    st = st.at[k]
    hidden = heads * 64
    qkv[...] = mm(n1[...], w[: 3 * hidden, :], NT).astype(BF)
    feat = unpack_feat(w[3 * hidden :, :])
    mask = causal(rows)
    for h in range(heads):
        fmap = head_map(feat, h)
        hl = slice(h * LANES, (h + 1) * LANES)
        for m in range(micro):
            rs = slice(m * rows, (m + 1) * rows)
            z = mm(qkv[rs, hl], fmap)
            pq = softmax_rows(z[:, :LANES]).astype(BF)
            pk = softmax_rows(z[:, LANES:]).astype(BF)
            phq[rs, hl] = pq
            phk[rs, hl] = pk
            v0 = heads * LANES + h * 64
            v1 = with_ones(qkv[rs, v0 : v0 + 64])
            prob = jnp.where(mask, mm(pq, pk, NT), 0.0).astype(BF)
            acc[rs, hl] = mm(prob, v1)
            put_state(st, m, h, heads, mm(v1, pk, TN))


def put_state(st, m, h, heads, lt):
    st[m, h * 64 : (h + 1) * 64, :] = lt[:64].astype(BF)
    base = heads * 64
    row = lax.broadcasted_iota(jnp.int32, (16, LANES), 0)
    mine = jnp.where(row == h, lt[64:80], 0.0)
    if h == 0:
        st[m, base : base + 16, :] = mine.astype(BF)
    else:
        st[m, base : base + 16, :] = (st[m, base : base + 16, :].astype(F32) + mine).astype(BF)


def take_state(s, h, heads):
    row = s[heads * 64 + h : heads * 64 + h + 1, :]
    return jnp.concatenate(
        [s[h * 64 : (h + 1) * 64, :], jnp.broadcast_to(row, (64, LANES))], axis=0
    ).astype(BF)


def relay_kernel(at, micro, meta, own, got, out):
    for m in range(micro):
        f = [meta[at + 4 * m + i].astype(F32) for i in range(2)]
        for k in range(SLOTS):
            out[k, m] = (f[0] * own[k, m].astype(F32) + f[1] * got[k ^ 1, m].astype(F32)).astype(BF)


def joined(at, meta, k, m, r1, r2):
    f = [meta[at + 4 * m + i].astype(F32) for i in (2, 3)]
    return f[0] * r1[k ^ 1, m].astype(F32) + f[1] * r2[k ^ 2, m].astype(F32)


def mix_kernel(rows, micro, heads, at, meta, x, gain, bias, r1, r2, *refs):
    accs, phqs, ws = refs[0:4], refs[4:8], refs[8:12]
    mixed, iden, ust, resid, n2 = refs[12:]
    hidden = heads * 64
    low = lane_low((rows, LANES))
    for m in range(micro):
        rs = slice(m * rows, (m + 1) * rows)
        for k in range(SLOTS):
            s = joined(at, meta, k, m, r1, r2)
            ust[k, m] = s.astype(BF)
            for h in range(heads):
                i = k * heads + h
                hl = slice(h * LANES, (h + 1) * LANES)
                a = accs[k][rs, hl] + mm(phqs[k][rs, hl], take_state(s, h, heads), NT)
                turned = pltpu.roll(a, 64, 1)
                if i % 2 == 0:
                    inv0 = 1.0 / turned
                    mix0 = a * inv0
                else:
                    inv1 = 1.0 / a
                    mix1 = turned * inv1
                    cl = slice((i // 2) * LANES, (i // 2 + 1) * LANES)
                    mixed[rs, cl] = jnp.where(low, mix0, mix1).astype(BF)
                    iden[rs, cl] = jnp.where(low, inv0, inv1)
    wo = jnp.concatenate([w[w.shape[0] - hidden :, :] for w in ws], axis=0)
    res = x[...].astype(F32) + mm(mixed[...], wo)
    resid[...] = res
    n, _ = norm_parts(res)
    n2[...] = (n * gain[1:2, :] + bias[1:2, :]).astype(BF)


def gelu_parts(u):
    a = 0.7978845608028654
    u2 = u * u
    t = jnp.tanh(a * u * (1.0 + 0.044715 * u2))
    half = 0.5 * (1.0 + t)
    return u * half, half + 0.5 * u * (1.0 - t * t) * a * (1.0 + 3 * 0.044715 * u2)


def mlp_kernel(k, first, meta, n2, g, u0, u1, d0, d1, *refs):
    if not first:
        mo_in, dn_in, *refs = refs
    keep, send, mo, dn = refs
    half = u1.shape[0]
    wu = jnp.concatenate([u0[:half, :], u1[...]], axis=0)
    wd = jnp.concatenate([d0[...], d1[...]], axis=0)
    up = mm(n2[...], wu, NT)
    hid, slope = gelu_parts(up)
    hid = hid.astype(BF)
    dup = (mm(g[...], wd, NT) * slope).astype(BF)
    a = mm(hid, wd)
    b = mm(dup, wu)
    mo[...] = a if first else mo_in[...] + a
    dn[...] = b if first else dn_in[...] + b
    mine = (meta[0] == 0) if k < 3 else True
    for at, grad in ((0, mm(dup, n2[...], TN)), (half, mm(hid, g[...], TN))):
        grad = grad.astype(BF)
        top, bottom = grad[:half], grad[half:]
        keep[at : at + half, :] = top if k == 3 else jnp.where(mine, top, bottom)
        send[at : at + half, :] = bottom if k == 3 else jnp.where(mine, bottom, top)


def turn_kernel(rows, micro, heads, meta, resid, mo, dn, g, gain, mixed, iden, *refs):
    phqs, ws = refs[0:4], refs[4:8]
    out, dres, dnx, gwo, hst, dln, dmix = refs[8:]
    hidden = heads * 64
    out[...] = (resid[...] + mo[...]).astype(BF)
    n, inverse = norm_parts(resid[...])
    a = dn[...]
    dr = g[...].astype(F32) + norm_back(a, n, inverse, gain[1:2, :])
    dres[...] = dr
    dln[...] = jnp.zeros_like(dln)
    dln[0:1, :] = jnp.sum(a * n, axis=0, keepdims=True)
    dln[1:2, :] = jnp.sum(a, axis=0, keepdims=True)
    dat = dr.astype(BF)
    gwo[...] = mm(mixed[...], dat, TN).astype(BF)
    wo = jnp.concatenate([w[w.shape[0] - hidden :, :] for w in ws], axis=0)
    dmix[...] = mm(dat, wo, NT)
    low = lane_low((rows, LANES))
    lane = lax.broadcasted_iota(jnp.int32, (LANES, 2 * LANES), 0) < 64
    column = lax.broadcasted_iota(jnp.int32, (LANES, 2 * LANES), 1) < LANES
    pick = jnp.where(lane == column, -1.0 / 64, 0.0).astype(BF)
    for m in range(micro):
        rs = slice(m * rows, (m + 1) * rows)
        for j in range(SLOTS * heads // 2):
            cl = slice(j * LANES, (j + 1) * LANES)
            d, iv = dmix[rs, cl], iden[rs, cl]
            t = d * mixed[rs, cl].astype(F32)
            both = mm(t.astype(BF), pick)
            even, odd = both[:, :LANES], both[:, LANES:]
            dn_ = d * iv
            x0 = jnp.where(low, dn_, even * pltpu.roll(iv, 64, 1)).astype(BF)
            x1 = jnp.where(low, pltpu.roll(dn_, 64, 1), odd * iv).astype(BF)
            for i, xv in ((2 * j, x0), (2 * j + 1, x1)):
                k, h = divmod(i, heads)
                hl = slice(h * LANES, (h + 1) * LANES)
                dnx[rs, i * LANES : (i + 1) * LANES] = xv
                put_state(hst.at[k], m, h, heads, mm(xv, phqs[k][rs, hl], TN))


def back_kernel(k, rows, micro, heads, meta, qkv, phq, phk, dnx, ust, wq, dpk, dv):
    mask = causal(rows)
    vbase = heads * LANES
    for h in range(heads):
        hl = slice(h * LANES, (h + 1) * LANES)
        dl = slice((k * heads + h) * LANES, (k * heads + h + 1) * LANES)
        for m in range(micro):
            rs = slice(m * rows, (m + 1) * rows)
            pq, pk, dx = phq[rs, hl], phk[rs, hl], dnx[rs, dl]
            v1 = with_ones(qkv[rs, vbase + h * 64 : vbase + h * 64 + 64])
            prob = jnp.where(mask, mm(pq, pk, NT), 0.0).astype(BF)
            ds = jnp.where(mask, mm(dx, v1, NT), 0.0).astype(BF)
            dpq = mm(ds, pk) + mm(dx, take_state(ust[k, m], h, heads))
            pqf = pq.astype(F32)
            wq[rs, hl] = (pqf * (dpq - jnp.sum(pqf * dpq, axis=-1, keepdims=True))).astype(BF)
            dpk[rs, hl] = mm(ds, pq, TN)
            dv[rs, hl] = mm(prob, dx, TN)


def last_kernel(k, rows, micro, heads, at, first, final, meta, qkv, phk, wq, dpk, dv, h1, h2, w, n1, gwo, *refs):
    if not first:
        dn1_in, *refs = refs
    if final:
        x, dres, gain, dln2, *refs = refs
        keep, send, gin, dln, dproj, ww, gw, dn1 = refs
    else:
        keep, send, dn1, dproj, ww, gw = refs
    hidden = heads * 64
    c = meta[0]
    feat = unpack_feat(w[3 * hidden :, :])
    feat_grads = []
    vbase = heads * LANES
    sts = [joined(at, meta, k, m, h1, h2) for m in range(micro)]
    for h in range(heads):
        fmap = head_map(feat, h)
        hl = slice(h * LANES, (h + 1) * LANES)
        for m in range(micro):
            rs = slice(m * rows, (m + 1) * rows)
            pk = phk[rs, hl]
            v1 = with_ones(qkv[rs, vbase + h * 64 : vbase + h * 64 + 64])
            hx = take_state(sts[m], h, heads)
            dp = dpk[rs, hl] + mm(v1, hx)
            dval = dv[rs, hl] + mm(pk, hx, NT)
            pkf = pk.astype(F32)
            wk = (pkf * (dp - jnp.sum(pkf * dp, axis=-1, keepdims=True))).astype(BF)
            wqk = jnp.concatenate([wq[rs, hl], wk], axis=1)
            ww[rs, :] = wqk
            dproj[rs, hl] = mm(wqk, fmap, NT).astype(BF)
            dproj[rs, vbase + h * 64 : vbase + h * 64 + 64] = dval[:, :64].astype(BF)
        g = mm(qkv[:, hl], ww[...], TN)
        top, bottom = g[:64], g[64:]
        gq = top[:, :LANES] - pltpu.roll(top[:, :LANES], 64, 1)
        gk = bottom[:, LANES:] - pltpu.roll(bottom[:, LANES:], 64, 1)
        feat_grads.append(jnp.where(lane_low(gq.shape), gq, -gk))
    total = mm(dproj[...], w[: 3 * hidden, :])
    dn1[...] = total if first else dn1_in[...] + total
    gw[...] = mm(dproj[...], n1[...], TN).astype(BF)
    fg = jnp.concatenate(feat_grads, axis=0)
    fg = jnp.concatenate([fg[i * 32 : (i + 1) * 32] for i in range(6)], axis=1).astype(BF)
    qh, oh = 3 * hidden // 2, hidden // 2
    for out, at in ((keep, c), (send, 1 - c)):
        out[:qh, :] = gw[pl.ds(pl.multiple_of(at * qh, 16), qh), :]
        out[qh : qh + oh, :] = gwo[pl.ds(pl.multiple_of(k * hidden + at * oh, 16), oh), :]
        out[qh + oh : qh + oh + 16, :] = jnp.where(at == 0, fg[:16], fg[16:])
        out[qh + oh + 16 :, :] = jnp.zeros_like(fg[:16])
    if final:
        n, inverse = norm_parts(x[...].astype(F32))
        a = dn1[...]
        gin[...] = dres[...] + norm_back(a, n, inverse, gain[0:1, :])
        dln[8:, :] = dln2[...]
        dln[:8, :] = jnp.zeros_like(dln2)
        dln[0:1, :] = jnp.sum(a * n, axis=0, keepdims=True)
        dln[1:2, :] = jnp.sum(a, axis=0, keepdims=True)


def split_kernel(terms, parts, meta, *refs):
    arrays, outs = refs[:terms], refs[terms:]
    z = meta[1]
    half = sum(out.shape[0] for out in outs[:parts])
    for side, group in ((z, outs[:parts]), (1 - z, outs[parts:])):
        at = side * half
        for out in group:
            n = out.shape[0]
            rs = pl.ds(pl.multiple_of(at, 16), n)
            total = arrays[0][rs, :].astype(F32)
            for t in arrays[1:]:
                total = total + t[rs, :].astype(F32)
            out[...] = total.astype(BF)
            at = at + n


def join_kernel(parts, meta, *refs):
    *pieces, out = refs
    half = out.shape[0] // 2
    for side, group in ((meta[1], pieces[:parts]), (1 - meta[1], pieces[parts:])):
        at = side * half
        for piece in group:
            n = piece.shape[0]
            out[pl.ds(pl.multiple_of(at, 16), n), :] = piece[...]
            at = at + n


def finish_ff_kernel(meta, own, other, gup_out, gdown_out, done, gup, gdown, sems):
    c = meta[0]
    half = own.shape[0] // 2
    is0 = c == 0
    first = jnp.where(is0, own[...], other[...])
    second = jnp.where(is0, other[...], own[...])
    gdown[:half, :] = first[half:].astype(F32)
    gdown[half:, :] = second[half:].astype(F32)
    down = pltpu.make_async_copy(gdown, gdown_out, sems.at[0])
    down.start()
    gup[...] = jnp.concatenate([first[:half], second[:half]], axis=0).astype(F32).T
    up = pltpu.make_async_copy(gup, gup_out, sems.at[1])
    up.start()
    done[...] = jnp.zeros_like(done)
    down.wait()
    up.wait()


def collect(meta, pieces, buf):
    c, z = meta[0], meta[1]
    quarter = pieces[0].shape[0]
    for piece, place in zip(pieces, (2 * c + z, 2 * c + 1 - z, 2 * (1 - c) + z, 2 * (1 - c) + 1 - z)):
        buf[pl.ds(pl.multiple_of(place * quarter, 16), quarter), :] = piece[...]


def finish_kernel(heads, meta, p0, p1, p2, p3, lns, more, gqkv, gfeat, gout, gains, biases, buf):
    collect(meta, (p0, p1, p2, p3), buf)
    hidden = heads * 64
    half, qh, oh = buf.shape[0] // 2, 3 * hidden // 2, hidden // 2

    def rows(at, n, first, size):
        parts = []
        while n:
            c, inner = divmod(at, size)
            m = min(n, size - inner)
            parts.append(buf[c * half + first + inner : c * half + first + inner + m, :])
            at, n = at + m, n - m
        return jnp.concatenate(parts, axis=0) if len(parts) > 1 else parts[0]

    for h in range(heads):
        for c in range(2):
            gqkv[c, h * 64 : (h + 1) * 64, :] = rows(h * LANES + c * 64, 64, 0, qh).astype(F32)
    gqkv[2] = rows(2 * hidden, hidden, 0, qh).astype(F32)
    gout[...] = rows(0, hidden, qh, oh).astype(F32)
    feat = unpack_feat(rows(0, 32, qh + oh, 16)).astype(F32)
    for h in range(heads):
        gfeat[0, h] = feat[h * 64 : (h + 1) * 64, :64]
        gfeat[1, h] = feat[h * 64 : (h + 1) * 64, 64:]
    ln = lns[...] + more[...]
    gains[0:1, :] = ln[0:1]
    gains[1:2, :] = ln[8:9]
    biases[0:1, :] = ln[1:2]
    biases[1:2, :] = ln[9:10]


def links(heads_axis, dp):
    def table(fn):
        return [(r * dp + d, q[0] * dp + q[1]) for r in range(heads_axis) for d in range(dp) for q in [fn(r, d)] if q]

    one = table(lambda r, d: (r ^ (1 + d % 2), d))
    two = table(lambda r, d: (r ^ (2 - d % 2), d))
    head = {b: table(lambda r, d: (r ^ b, d)) for b in (1, 2)}
    bits = {}
    b = 1
    while b < dp:
        bits[b] = table(lambda r, d: (r, d ^ b))
        b *= 2
    return one, two, head, bits


def move(v, table, name="move"):
    with jax.named_scope(name):
        return lax.ppermute(v, AXES, table)


def factors(r, core, keep):
    high, odd = r // 2, r % 2
    first = [jnp.ones_like(r), jnp.ones_like(r), odd, high * keep]
    second = [1 - high * odd, keep * high, keep * high, jnp.minimum(r, 1)]
    return [jnp.where(core == 0, a, b) for a, b in zip(first, second)]


def local(heads_axis, dp, block_in, ln_gains, ln_biases, w_qkv, feat_maps, w_out, w_up, w_down, seq_lengths, out_cotangent):
    one, two, head, bits = links(heads_axis, dp)
    micro, rows, width = block_in.shape[1:]
    tokens = micro * rows
    heads = feat_maps.shape[1]
    ff = w_up.shape[1]
    hidden = heads * 64
    rank, dpi = lax.axis_index("head"), lax.axis_index("dp")
    core, zbit = dpi % 2, (dpi // 2) % 2
    keeps = [1 - (seq_lengths[0, m, 1] > 0).astype(jnp.int32) for m in range(micro)]
    scalars = [core, zbit]
    for r in (rank, 3 - rank):
        for m in range(micro):
            scalars += factors(r, core, keeps[m])
    meta = jnp.stack([jnp.asarray(v, jnp.int32) for v in scalars])
    fwd, bwd = 2, 2 + 4 * micro

    x = block_in.reshape(tokens, width)
    g = out_cotangent.reshape(tokens, width)
    tw = (tokens, width)

    arows, half = 3 * hidden + 32, ff // 2
    call = Order()
    swap = lambda v, name="swap": move(v, bits[1], name)
    piece = ((half, width), BF)

    (a0,) = call(partial(pack_kernel, heads), [jnp.swapaxes(w_qkv, 1, 2), feat_maps], [((arows, width), BF)], meta=False)
    a1 = move(a0, one, "a1")
    u0, u1 = call(turn_over_kernel, [w_up, w_out], [((half + hidden, width), BF), piece], meta=False)
    bu0 = move(u0, one, "bu0")

    wl, qw = heads * LANES, 3 * hidden
    st_all = (SLOTS, micro, hidden + 16, LANES)
    first_outs = [((tokens, qw), BF), ((tokens, wl), BF), ((tokens, wl), BF), ((tokens, wl), F32), (st_all, BF)]
    first = lambda k: partial(first_kernel, k, rows, micro, heads)
    slots = []

    def attend(k, w):
        slots.append(call(first(k), [meta, n1, w, slots[-1][4]], first_outs, alias={3: 4}, limit=16))

    n1, *slot = call(first(0), [meta, x, ln_gains, ln_biases, a0], [(tw, BF)] + first_outs, limit=16)
    slots.append(slot)
    a1 = call.gate(a1)
    a2 = swap(a1, "a2")
    (asl,) = call(pick_half_kernel, [meta, a1], [((arows // 2, width), BF)])
    ahalf = move(asl, two, "ahalf")
    u1 = call.gate(u1)
    bu1 = move(u1, one, "bu1")
    d0, d1 = call(copy_kernel, [w_down], [piece] * 2, meta=False)
    attend(1, a1)
    d0 = call.gate(d0)
    bd0 = move(d0, one, "bd0")
    attend(2, a2)
    ahalf = call.gate(ahalf)
    aother = swap(ahalf, "aother")
    bu0 = call.gate(bu0)
    b2u0 = swap(bu0, "b2u0")
    (wo1,) = call(tail_kernel, [bu0], [((hidden, width), BF)], meta=False)
    wo3 = move(wo1, two, "wo3")
    a3, *slot = call(
        first(3), [meta, n1, ahalf, aother, slots[-1][4]], [((arows, width), BF)] + first_outs, alias={4: 5}, limit=16
    )
    slots.append(slot)
    ws = [a0, a1, a2, a3]
    qkvs, phqs, phks, accs, sts = zip(*slots)

    r1 = move(sts[-1], one, "r1")
    bu1, d1, wo3 = call.gate(bu1, d1, wo3)
    b2u1 = swap(bu1, "b2u1")
    bd1 = move(d1, one, "bd1")
    (du,) = call(pick_kernel, [meta, bu0, bu1], [piece])
    (on,) = call(partial(relay_kernel, fwd, micro), [meta, sts[-1], r1], [(st_all, BF)])
    r2 = move(on, two, "r2")
    bd0, b2u1, b2u0, du = call.gate(bd0, b2u1, b2u0, du)
    wouts = [w_out, bu0, b2u0, wo3]
    b2d0 = swap(bd0, "b2d0")
    du = move(du, two, "du")
    call.pause()
    r2, bd1 = call.gate(r2, bd1)
    b2d1 = swap(bd1, "b2d1")
    (dd,) = call(pick_kernel, [meta, bd0, bd1], [piece])
    dd = move(dd, two, "dd")
    b2d0 = call.gate(b2d0)
    mixed, iden, ust, resid, n2 = call(
        partial(mix_kernel, rows, micro, heads, fwd),
        [meta, x, ln_gains, ln_biases, r1, r2, *accs, *phqs, *wouts],
        [(tw, BF), (tw, F32), (st_all, BF), (tw, F32), (tw, BF)],
        limit=24,
    )

    keeps, sends = [None] * SLOTS, [None] * SLOTS
    sums = []

    def mlp(k, *w):
        keeps[k], sends[k], *sums[:] = call(
            partial(mlp_kernel, k, not sums),
            [meta, n2, g, *w, *sums],
            [((ff, width), BF), ((ff, width), BF), (tw, F32), (tw, F32)],
            alias={7: 2, 8: 3} if sums else None,
            limit=16,
        )
        return swap(sends[k], "got%d" % k)

    def split(terms, sizes, names):
        w = terms[0].shape[1]
        outs = [((n, w), BF) for n in sizes] * 2
        res = call(partial(split_kernel, len(terms), len(sizes)), [meta, *terms], outs)
        n = len(sizes)
        return [(res[i], move(res[n + i], bits[2], names[i])) for i in reversed(range(n))][::-1]

    got1 = mlp(1, bu0, bu1, bd0, bd1)
    got2 = mlp(2, b2u0, b2u1, b2d0, b2d1)
    du, dd = call.gate(du, dd)
    du2, dd2 = swap(du, "du2"), swap(dd, "dd2")
    got0 = mlp(0, u0, u1, d0, d1)
    s1 = call.add(keeps[1], got2)
    one1 = move(s1, one, "one1")
    chunk = ((ff // 2, width), BF)
    s2 = call(add_chunks_kernel, [keeps[2], got1], [chunk] * 2, meta=False)
    got3 = mlp(3, du, du2, dd, dd2)
    mo, dn = sums

    out, dres, dnx, gwo, hst, dln2 = call(
        partial(turn_kernel, rows, micro, heads),
        [meta, resid, mo, dn, g, ln_gains, mixed, iden, *phqs, *wouts],
        [(tw, BF), (tw, F32), ((tokens, SLOTS * wl), BF), ((SLOTS * hidden, width), BF), (st_all, BF), ((8, width), F32)],
        scratch=[pltpu.VMEM(tw, F32)],
        limit=24,
    )
    h1 = move(hst, one, "h1")
    (s3a,) = call(partial(add_chunk_kernel, 0), [keeps[3], got3], [chunk], meta=False)
    one3a = move(s3a, one, "one3a")
    backs = []

    def back(k):
        backs.append(
            call(
                partial(back_kernel, k, rows, micro, heads),
                [meta, qkvs[k], phqs[k], phks[k], dnx, ust],
                [((tokens, wl), BF), ((tokens, wl), F32), ((tokens, wl), F32)],
                limit=16,
            )
        )

    back(0)
    s0 = call.add(keeps[0], got0)
    back(1)
    (on,) = call(partial(relay_kernel, bwd, micro), [meta, hst, h1], [(st_all, BF)])
    h2 = move(on, two, "h2")
    p = call(add_chunks_kernel, [s0, one1], [chunk] * 2, meta=False)
    back(2)
    (s3b,) = call(partial(add_chunk_kernel, 1), [keeps[3], got3], [chunk], meta=False)
    one3b = move(s3b, one, "one3b")
    back(3)
    q = call.add(s2[0], one3a)
    two2a = move(q, two, "two2a")

    grows = 4 * hidden + 64
    akeeps, asends = [None] * SLOTS, [None] * SLOTS
    dn1 = []

    def last(k):
        final = k == 0
        args = [meta, qkvs[k], phks[k], *backs[k], h1, h2, ws[k], n1, gwo, *dn1]
        outs = [((grows // 2, width), BF)] * 2
        scratch = [pltpu.VMEM((tokens, qw), BF), pltpu.VMEM((tokens, 2 * LANES), BF), pltpu.VMEM((qw, width), BF)]
        akeeps[k], asends[k], *dn1[:] = call(
            partial(last_kernel, k, rows, micro, heads, bwd, not dn1, final),
            args + ([x, dres, ln_gains, dln2] if final else []),
            outs + ([(tw, F32), ((16, width), F32)] if final else [(tw, F32)]),
            scratch=scratch + ([pltpu.VMEM(tw, F32)] if final else []),
            alias={11: 2} if dn1 and not final else None,
            limit=18,
        )
        return swap(asends[k], "agot%d" % k)

    agot3 = last(3)
    agot1 = last(1)
    q = call.add(s2[1], one3b)
    two2b = move(q, two, "two2b")
    t3 = call.add(akeeps[3], agot3)
    aone3 = move(t3, one, "aone3")
    agot2 = last(2)
    (f0,) = split([p[0], two2a], [ff // 4], ["zf0"])
    t2 = call.add(akeeps[2], agot1)
    t1 = call.add(akeeps[1], agot2)
    aone1 = move(t1, one, "aone1")
    agot0 = last(0)
    gin, lns = dn1
    t2 = call.add(t2, aone3)
    atwo2 = move(t2, two, "atwo2")

    zs = [b for b in sorted(bits) if b > 2]
    (f1,) = split([p[1], two2b], [ff // 4], ["zf1"])
    f0 = call.add(*f0)
    if zs:
        f0 = (f0, move(f0, bits[zs[0]], "yf0"))
    t0 = call.add(akeeps[0], agot0)
    steps = [bits[b] for b in sorted(bits) if b > 1] + [bits[1], one, two]
    lns = call.gate(lns)
    ln = move(lns, steps.pop(0), "ln")

    def more_norms():
        nonlocal lns, ln
        lns = call.add(lns, ln)
        ln = move(lns, steps.pop(0), "ln")

    (at,) = split([t0, aone1, atwo2], [grows // 4], ["za"])
    call.pause()
    f1 = call.add(*f1)
    if zs:
        f1 = (f1, move(f1, bits[zs[0]], "yf1"))
    for b in zs[1:]:
        f0, f1 = [call.add(*v) for v in (f0, f1)]
        f0, f1 = [(v, move(v, bits[b])) for v in (f0, f1)]
    f0 = call.add(*f0) if zs else f0
    xf0 = move(f0, bits[2], "xf0")
    at = call.add(*at)
    if zs:
        at = (at, move(at, bits[zs[0]], "ya"))
    more_norms()
    if zs:
        f1 = call.add(*f1)
    xf1 = move(f1, bits[2], "xf1")
    if zs:
        at = call.add(*at)
    for b in zs[1:]:
        at = call.add(at, move(at, bits[b]))
    xa = move(at, bits[2], "xa")
    am = swap(at, "am")
    more_norms()
    call.pause()
    more_norms()
    (ffh,) = call(partial(join_kernel, 2), [meta, f0, f1, xf0, xf1], [((ff, width), BF)])
    ffo = swap(ffh, "ffo")
    while steps:
        more_norms()
    gup, gdown, _ = call(
        finish_ff_kernel,
        [meta, ffh, ffo],
        [((width, ff), F32), ((ff, width), F32), ((8, LANES), F32)],
        scratch=[pltpu.VMEM((width, ff), F32), pltpu.VMEM((ff, width), F32), pltpu.SemaphoreType.DMA((2,))],
        limit=16,
        place=[HBM, HBM, VMEM],
    )
    xa = call.gate(xa)
    ax = swap(xa, "ax")
    call.pause()
    gqkv, gfeat, gout, gains, biases = call(
        partial(finish_kernel, heads),
        [meta, at, xa, am, ax, lns, ln],
        [((3, hidden, width), F32), (feat_maps.shape, F32), (w_out.shape, F32), (ln_gains.shape, F32), (ln_biases.shape, F32)],
        scratch=[pltpu.VMEM((grows, width), BF)],
    )
    gqkv = jnp.swapaxes(gqkv, 1, 2)
    shape = (1, micro, rows, width)
    return (out.reshape(shape), gin.reshape(shape), gains, biases, gqkv, gfeat, gout, gup, gdown)


def solution(mesh):
    return jax.shard_map(
        partial(local, mesh.shape["head"], mesh.shape["dp"]),
        mesh=mesh,
        in_specs=(
            P("dp", None, "head", None),
            P(),
            P(),
            P(None, None, "head"),
            P(None, "head", None, None),
            P("head", None),
            P(None, "head"),
            P("head", None),
            P("dp", None, None),
            P("dp", None, "head", None),
        ),
        out_specs=(
            P("dp", None, "head", None),
            P("dp", None, "head", None),
            P(),
            P(),
            P(None, None, "head"),
            P(None, "head", None, None),
            P("head", None),
            P(None, "head"),
            P("head", None),
        ),
        check_vma=False,
    )
```
